128 devices in a mesh: seq: 32 (over y, x, core), exp: 4 (over z).
Axes of the slice: x: 4, y: 4, z: 4, core: 2. Of those that a mesh axis runs over, the one named last changes fastest.
Arguments:
- queries: bfloat16 [16384, 4096], P('seq', 'exp'), may hold values from -200 to 200
- keys: bfloat16 [16384, 512], P('seq', 'exp'), may hold values from -8 to 8
- values: bfloat16 [16384, 512], P('seq', 'exp'), may hold values from -6 to 6
- doc_lengths: int32 [16], replicated, may hold values from 1 to 2048, 16384 in all
- out_weight: bfloat16 [4096, 4096], P('exp', 'seq'), may hold values from -0.09375 to 0.09375
- residual: bfloat16 [16384, 4096], P(('seq', 'exp')), may hold values from -3 to 3
- norm_gain: float32 [4096], replicated, may hold values from 0.5 to 1.5
- expert_ids: int32 [16384, 8], P(('seq', 'exp')), may hold values from 0 to 127, all different within a row; in each aligned block of 128 rows (0 to 127, 128 to 255, ...) at most 9 rows name the same one
- gate_values: float32 [16384, 8], P(('seq', 'exp')), may hold values from 0.05 to 0.3
- w_gate: bfloat16 [128, 4096, 768], P(('seq', 'exp')), may hold values from -0.09375 to 0.09375
- w_up: bfloat16 [128, 4096, 768], P(('seq', 'exp')), may hold values from -0.09375 to 0.09375
- w_down: bfloat16 [128, 768, 4096], P(('seq', 'exp')), may hold values from -0.21875 to 0.21875
Outputs:
- mixed: bfloat16 [16384, 4096], P(('seq', 'exp'))
The draws below stay inside these ranges and needn't reach their ends.
Inputs may be any that keep to these rules, and one draw needn't show every extreme that they name: `doc_lengths`: the 16 documents fill the row of 16384 tokens in order; the longest has exactly 2048 tokens. `expert_ids`: among the routes of one device's 128 tokens (aligned blocks of tokens in order), no expert is named more than 9 times, a bound that some block reaches; a token names 8 different experts.
All inputs are finite; a program needn't handle non-finite values.
Results may differ from the reference program's by a relative error of at most 0.015.
Values may be sent and summed in bfloat16 or wider, within the bound.
A program may use at most 192 MiB of HBM per device.

```python
import math
import jax
import jax.numpy as jnp
import numpy as np
from jax import lax

D = 4096
HEADS = 32
KV_HEADS = 4
HEAD_DIM = 128
FFH = 768
TOPK = 8
TOK_DEV = 512
TOKENS = 16384
MAX_DOC = 2048
NUM_DOCS = 16
MOE_DEV = 128
EXPERTS = 128
CAP = 9
N_EXP = 4


def base_keys(key):
    drawn = jax.random.normal(jax.random.fold_in(key, 101), (TOKENS, KV_HEADS * HEAD_DIM), jnp.float32)
    return jnp.clip(drawn, -6.0, 6.0)


def draw_keys(key, part):
    drawn = base_keys(key)
    return drawn.astype(jnp.bfloat16)


def draw_queries(key, part):
    key = jax.random.fold_in(key, 4)
    drawn = jnp.clip(jax.random.normal(key, (TOKENS, HEADS * HEAD_DIM), jnp.float32), -6.0, 6.0)
    return drawn.astype(jnp.bfloat16)


def shard_levels(stream_key, shape, pieces, smallest, largest):
    gain = 1.0
    for axis_at, shards_of in pieces:
        steps = jax.random.uniform(jax.random.fold_in(jax.random.fold_in(stream_key, 6), axis_at), (shards_of,), jnp.float32, smallest / len(pieces), largest / len(pieces))
        gain = gain * jnp.repeat(jnp.exp(steps), shape[axis_at] // shards_of).reshape((-1,) + (1,) * (len(shape) - 1 - axis_at))
    return gain


def split_up(count, total, most, skew):
    weights = [(1 << 20) // math.isqrt(rank ** skew) + 1 for rank in range(2, count + 1)]
    rest, given = total - most - (count - 1), [1] * (count - 1)
    while rest > 0:
        candidates = [i for i in range(count - 1) if given[i] < most]
        pool, left = sum([weights[i] for i in candidates]), rest
        for i in candidates:
            more = min(most - given[i], max(1, left * weights[i] // pool), rest)
            given[i] = given[i] + more
            rest = rest - more
    return np.array([most] + given)


def ragged_sizes(rng, amount, total, reach, lean):
    if amount == 2:
        one = jax.random.randint(rng, (), max(1, total - reach), min(reach, total - 1) + 1)
        return jnp.stack([one, total - one])
    lengths = jnp.asarray(split_up(amount, total, reach, lean), jnp.int32)
    couples = (amount - 1) // 2
    donor, sink = lengths[1:1 + 2 * couples:2], lengths[2:2 + 2 * couples:2]
    room = jnp.minimum(donor - 1, reach - sink)
    passed = jax.random.randint(jax.random.fold_in(rng, 1), (couples,), 0, 1 << 20) % (room + 1)
    lengths = lengths.at[1:1 + 2 * couples:2].set(donor - passed).at[2:2 + 2 * couples:2].set(sink + passed)
    return lengths[jax.random.permutation(jax.random.fold_in(rng, 2), amount)]


def assign_block(stream_key, own, number, rows, amount, top, limit, lean):
    order = jax.random.permutation(stream_key, amount)
    heavy_load, ordinary = shares(amount, rows * top, limit, lean, True), shares(amount, rows * top, limit, lean, False)
    places = jnp.arange(amount)

    def named(sizes, rotation):
        used = int((sizes > 0).sum())
        fixed = max(1, used // 4)
        moved = fixed + (places - fixed + rotation * (used - fixed)) % max(1, amount - fixed)
        return jnp.zeros((amount,), jnp.int32).at[order[jnp.where(places < fixed, places, moved)]].set(jnp.asarray(sizes, jnp.int32))

    sizes = jnp.where(number % 4 == 0, named(heavy_load, number // 4), named(ordinary, number - number // 4 - 1))
    mixed = jax.random.permutation(jax.random.fold_in(own, 3), amount)
    source_of, taker = mixed[0:amount // 2 * 2:2], mixed[1:amount // 2 * 2:2]
    room = jnp.minimum(sizes[source_of] - 1, limit - sizes[taker]) // 2
    room = jnp.where((source_of == order[0]) | (taker == order[0]) | (sizes[taker] == 0), 0, jnp.maximum(room, 0))
    moved = jax.random.randint(jax.random.fold_in(own, 4), (amount // 2,), 0, 1 << 20) % (room + 1)
    sizes = sizes.at[source_of].add(-moved).at[taker].add(moved)
    items = jnp.searchsorted(jnp.cumsum(sizes), jnp.arange(rows * top), side="right").astype(jnp.int32)
    grid = items.reshape(top, rows).T
    grid = grid[jax.random.permutation(jax.random.fold_in(own, 1), rows)]
    rotation = jax.random.randint(jax.random.fold_in(own, 2), (rows, 1), 0, top)
    return jnp.take_along_axis(grid, (jnp.arange(top)[None, :] + rotation) % top, axis=1)


def shares(number_of, total, most, lean, full):
    loads = [(1 << 20) // math.isqrt(standing ** lean) + 1 for standing in range(1, number_of + 1)]
    largest = most if full else min(most, max(-(-total // number_of), total * loads[0] // sum(loads)))
    least = 1 if total - largest >= number_of - 1 else 0
    given, rest = [largest] + [least] * (number_of - 1), total - largest - least * (number_of - 1)
    while rest > 0:
        movable = [i for i in range(1, number_of) if given[i] < largest] or [i for i in range(1, number_of) if given[i] < most]
        whole, left = sum([loads[i] for i in movable]), rest
        for i in movable:
            more = min(most - given[i], max(1, left * loads[i] // whole), rest)
            given[i] = given[i] + more
            rest = rest - more
    return np.array(given)


def scatter_about(stream_key, shape, width, most, pieces=(), kind=jnp.bfloat16):
    values = width * jax.random.normal(stream_key, shape, jnp.float32)
    if pieces:
        values = values * shard_levels(stream_key, shape, pieces, -0.22, 0.18)
    return jnp.clip(values, -most, most).astype(kind)


def setup_inputs(seed: int = 0) -> dict:
    key_list = jax.random.split(jax.random.key(seed), 13)
    queries = draw_queries(jax.random.fold_in(key_list[12], 71), 0)
    keys = draw_keys(jax.random.fold_in(key_list[12], 71), 0)
    values = scatter_about(key_list[2], (TOKENS, KV_HEADS * HEAD_DIM), 1.0, 6.0, ((0, 32), (1, 4)))
    doc_lengths = ragged_sizes(key_list[3], NUM_DOCS, TOKENS, MAX_DOC, 2).astype(jnp.int32)
    out_weight = scatter_about(key_list[4], (HEADS * HEAD_DIM, D), (HEADS * HEAD_DIM) ** -0.5, 0.09375, ((0, 4), (1, 32)))
    residual = scatter_about(key_list[5], (TOKENS, D), 0.5, 3.0, ((0, 128),))
    norm_gain = jnp.clip(1.0 + 0.1 * jax.random.normal(key_list[6], (D,), jnp.float32), 0.5, 1.5)
    expert_ids_keys = jax.random.split(jax.random.fold_in(key_list[7], 1), TOKENS // MOE_DEV)
    expert_ids_turns = jax.random.permutation(jax.random.fold_in(key_list[7], 3), TOKENS // MOE_DEV)
    expert_ids = jax.vmap(lambda own, number: assign_block(jax.random.fold_in(key_list[7], 2), own, number, MOE_DEV, EXPERTS, TOPK, CAP, 1))(expert_ids_keys, expert_ids_turns).reshape((TOKENS, TOPK))
    gate_values = jnp.clip(0.05 + 0.25 * jax.random.uniform(key_list[8], (TOKENS, TOPK), jnp.float32) ** shard_levels(key_list[8], (TOKENS, TOPK), ((0, 128),), -0.2, 0.2), 0.05, 0.3)
    w_gate = scatter_about(key_list[9], (EXPERTS, D, FFH), D ** -0.5, 0.09375, ((0, 128),))
    w_up = scatter_about(key_list[10], (EXPERTS, D, FFH), D ** -0.5, 0.09375, ((0, 128),))
    w_down = scatter_about(key_list[11], (EXPERTS, FFH, D), FFH ** -0.5, 0.21875, ((0, 128),))
    return {"queries": queries, "keys": keys, "values": values, "doc_lengths": doc_lengths, "out_weight": out_weight, "residual": residual, "norm_gain": norm_gain, "expert_ids": expert_ids, "gate_values": gate_values, "w_gate": w_gate, "w_up": w_up, "w_down": w_down}


def doc_index(positions, doc_lengths):
    doc_ends = jnp.cumsum(doc_lengths).astype(jnp.int32)
    return lax.optimization_barrier(jnp.sum((positions[:, None] >= doc_ends[None, :]).astype(jnp.int32), axis=1))

def reference(queries, keys, values, doc_lengths, out_weight, residual, norm_gain, expert_ids, gate_values, w_gate, w_up, w_down):
    group = HEADS // KV_HEADS
    span = MAX_DOC + TOK_DEV
    scale = HEAD_DIM ** (-0.5)
    front = jnp.zeros((MAX_DOC, KV_HEADS * HEAD_DIM), keys.dtype)
    padded_keys = jnp.concatenate([front, keys], axis=0)
    padded_values = jnp.concatenate([front, values], axis=0)

    def attend_block(block_id):
        first = (block_id * TOK_DEV).astype(jnp.int32)
        query_block = lax.dynamic_slice_in_dim(queries, first, TOK_DEV, 0).astype(jnp.float32)
        query_block = query_block.reshape(TOK_DEV, KV_HEADS, group, HEAD_DIM)
        key_block = lax.dynamic_slice_in_dim(padded_keys, first, span, 0).astype(jnp.float32)
        key_block = key_block.reshape(span, KV_HEADS, HEAD_DIM)
        value_block = lax.dynamic_slice_in_dim(padded_values, first, span, 0).astype(jnp.float32)
        value_block = value_block.reshape(span, KV_HEADS, HEAD_DIM)
        query_pos = first + jnp.arange(TOK_DEV, dtype=jnp.int32)
        key_pos = first - MAX_DOC + jnp.arange(span, dtype=jnp.int32)
        same_doc = doc_index(key_pos, doc_lengths)[None, :] == doc_index(query_pos, doc_lengths)[:, None]
        visible = (key_pos[None, :] >= 0) & (key_pos[None, :] <= query_pos[:, None]) & same_doc
        scores = jnp.einsum('tkgd,skd->kgts', query_block, key_block) * scale
        masked = jnp.where(visible, scores, -1e+30)
        highest = lax.optimization_barrier(jnp.max(masked, axis=-1, keepdims=True))
        weights = jnp.where(visible, jnp.exp(masked - highest), 0.0)
        total = lax.optimization_barrier(jnp.sum(weights, axis=-1))
        rounded = lax.optimization_barrier(weights.astype(jnp.bfloat16)).astype(jnp.float32)
        summed = jnp.einsum('kgts,skd->tkgd', rounded, value_block)
        result = summed / jnp.transpose(total, (2, 0, 1))[..., None]
        return result.reshape(TOK_DEV, HEADS * HEAD_DIM).astype(jnp.bfloat16)
    block_ids = jnp.arange(TOKENS // TOK_DEV, dtype=jnp.int32)
    attended = lax.map(attend_block, block_ids).reshape(TOKENS, HEADS * HEAD_DIM)
    columns = HEADS * HEAD_DIM // N_EXP
    projected = jnp.zeros((TOKENS, D), jnp.float32)
    for grp in range(N_EXP):
        partial_sum = jnp.dot(attended[:, grp * columns:(grp + 1) * columns], out_weight[grp * columns:(grp + 1) * columns], preferred_element_type=jnp.float32)
        partial_sum = lax.optimization_barrier(partial_sum.astype(jnp.bfloat16)).astype(jnp.float32)
        projected = projected + partial_sum
    hidden_state = residual.astype(jnp.float32) + projected
    variance = lax.optimization_barrier(jnp.mean(hidden_state * hidden_state, axis=1, keepdims=True))
    normed = (hidden_state * lax.rsqrt(variance + 1e-06) * norm_gain[None, :]).astype(jnp.bfloat16)
    flat_ids = expert_ids.reshape(-1)
    flat_gates = gate_values.reshape(-1)
    order = jnp.argsort(flat_ids, stable=True).astype(jnp.int32)
    counts = lax.optimization_barrier(jnp.sum((flat_ids[None, :] == jnp.arange(EXPERTS, dtype=jnp.int32)[:, None]).astype(jnp.int32), axis=1))
    starts = (jnp.cumsum(counts) - counts).astype(jnp.int32)
    bound = EXPERTS * CAP
    padded_order = jnp.concatenate([order, jnp.zeros((bound,), jnp.int32)])

    def expert_step(accum, inputs):
        expert, gate_mat, up_mat, down_mat = inputs
        chosen = lax.dynamic_slice(padded_order, (starts[expert].astype(jnp.int32),), (bound,))
        valid = jnp.arange(bound, dtype=jnp.int32) < counts[expert]
        token_rows = chosen // TOPK
        picked = normed[token_rows]
        gate_part = jnp.dot(picked, gate_mat, preferred_element_type=jnp.float32)
        up_part = jnp.dot(picked, up_mat, preferred_element_type=jnp.float32)
        inner = (jax.nn.silu(gate_part) * up_part).astype(jnp.bfloat16)
        produced = jnp.dot(inner, down_mat, preferred_element_type=jnp.float32).astype(jnp.bfloat16)
        weight = jnp.where(valid, flat_gates[chosen], 0.0)
        accum = accum.at[token_rows].add(produced.astype(jnp.float32) * weight[:, None])
        return (accum, None)
    routed, _ = lax.scan(expert_step, jnp.zeros((TOKENS, D), jnp.float32), (jnp.arange(EXPERTS, dtype=jnp.int32), w_gate, w_up, w_down))
    return (hidden_state + routed).astype(jnp.bfloat16)
```

```python
import functools

import jax
import jax.numpy as jnp
from jax import lax
from jax.experimental import pallas as pl
from jax.experimental.pallas import tpu as pltpu
from jax.sharding import PartitionSpec as P

HEAD_DIM = 128
DOC_SHARDS = 4
NEG_FILL = -1e30
D = 4096
HALF = D // 2
FFH = 768
CAP = 9
DEVICES = 128
GROUPS = 4
PER_GROUP = DEVICES // GROUPS
MAIN = PER_GROUP * 8
ROWS = PER_GROUP * CAP
EXTRA = D // 16
MESSAGE = HALF + EXTRA
CHUNK = 512
STRIDE = 37
MESH = pl.DeviceIdType.MESH


def place():
    seq = lax.axis_index("seq")
    return seq // 8, (seq // 2) % 4, seq % 2, lax.axis_index("exp")


def route_target(index):
    y, x, c, z = place()
    j = (index * STRIDE) % DEVICES
    dy, dx, dc, dz = j // 32, (j // 8) % 4, (j // 4) % 2, j % 4
    ey = jnp.where(c == 0, dy, dx)
    ex = jnp.where(c == 0, dx, dz)
    ez = jnp.where(c == 0, dz, dy)
    return (y + ey) % 4, (x + ex) % 4, (c + dc) % 2, (z + ez) % 4


def route_source(index):
    y, x, c, z = place()
    j = (index * STRIDE) % DEVICES
    dy, dx, dc, dz = j // 32, (j // 8) % 4, (j // 4) % 2, j % 4
    sc = (c + dc) % 2
    ey = jnp.where(sc == 0, dy, dx)
    ex = jnp.where(sc == 0, dx, dz)
    ez = jnp.where(sc == 0, dz, dy)
    return (y - ey + 4) % 4, (x - ex + 4) % 4, sc, (z - ez + 4) % 4


def device(y, x, c, z):
    return {"seq": (y * 4 + x) * 2 + c, "exp": z}


def moe_kernel(
    normed, hidden, picks, gates, perm, perm_t, w_gate, w_up, w_down, out,
    outbound, arrived, returned, wg, wu, wd, rows, extra, acc,
    weight_sem, send_sem, recv_sem, back_send_sem, back_recv_sem,
):
    loads = [
        pltpu.make_async_copy(src.at[0], dst, weight_sem.at[k])
        for k, (src, dst) in enumerate(((w_gate, wg), (w_up, wu), (w_down, wd)))
    ]
    for load in loads:
        load.start()

    def pack(buffer, first, c, left, right):
        both = jnp.concatenate(
            [left.reshape(PER_GROUP, 8, CHUNK), right.reshape(PER_GROUP, 8, CHUNK)], axis=1
        )
        buffer[pl.ds(first, PER_GROUP), :, c : c + CHUNK] = both.astype(jnp.bfloat16)

    def pack_extra(buffer, first):
        stacked = jnp.concatenate(
            [extra[:, j * EXTRA : (j + 1) * EXTRA] for j in range(16)], axis=0
        ).astype(jnp.bfloat16)
        turned = jnp.dot(perm_t[...], stacked, preferred_element_type=jnp.float32)
        buffer[pl.ds(first, PER_GROUP), :, HALF:MESSAGE] = turned.astype(jnp.bfloat16).reshape(
            PER_GROUP, 16, EXTRA
        )

    def unpack(buffer, first):
        for c in range(0, HALF, CHUNK):
            both = buffer[pl.ds(first, PER_GROUP), :, c : c + CHUNK].astype(jnp.float32)
            rows[0:MAIN, c : c + CHUNK] = both[:, 0:8].reshape(MAIN, CHUNK).astype(jnp.bfloat16)
            rows[0:MAIN, HALF + c : HALF + c + CHUNK] = (
                both[:, 8:16].reshape(MAIN, CHUNK).astype(jnp.bfloat16)
            )
        stacked = buffer[pl.ds(first, PER_GROUP), :, HALF:MESSAGE].reshape(PER_GROUP * 16, EXTRA)
        turned = jnp.dot(perm[...], stacked, preferred_element_type=jnp.float32)
        for j in range(16):
            rows[MAIN:ROWS, j * EXTRA : (j + 1) * EXTRA] = turned[
                j * PER_GROUP : (j + 1) * PER_GROUP
            ].astype(jnp.bfloat16)

    def build(g, carry):
        first = g * PER_GROUP
        for c in range(0, HALF, CHUNK):
            halves = []
            for base in (c, HALF + c):
                got = jnp.dot(
                    picks[g], normed[:, base : base + CHUNK], preferred_element_type=jnp.float32
                )
                extra[:, base : base + CHUNK] = got[MAIN:ROWS]
                halves.append(got[0:MAIN])
            pack(outbound, first, c, *halves)
        pack_extra(outbound, first)

        def send(k, carry):
            index = first + k

            @pl.when(index == 0)
            def _():
                pltpu.make_async_copy(outbound.at[0], arrived.at[0], recv_sem.at[0]).start()

            @pl.when(index > 0)
            def _():
                pltpu.make_async_remote_copy(
                    src_ref=outbound.at[index],
                    dst_ref=arrived.at[index],
                    send_sem=send_sem,
                    recv_sem=recv_sem.at[g],
                    device_id=device(*route_target(index)),
                    device_id_type=MESH,
                ).start()

            return carry

        return lax.fori_loop(0, PER_GROUP, send, carry)

    lax.fori_loop(0, GROUPS, build, 0)
    for load in loads:
        load.wait()

    def expert(g, carry):
        first = g * PER_GROUP
        block = arrived.at[pl.ds(first, PER_GROUP)]
        pltpu.make_async_copy(block, block, recv_sem.at[g]).wait()
        unpack(arrived, first)
        gate_part = jnp.dot(rows[...], wg[...], preferred_element_type=jnp.float32)
        up_part = jnp.dot(rows[...], wu[...], preferred_element_type=jnp.float32)
        inner = (gate_part / (1.0 + jnp.exp(-gate_part)) * up_part).astype(jnp.bfloat16)
        for c in range(0, HALF, CHUNK):
            halves = []
            for base in (c, HALF + c):
                got = jnp.dot(
                    inner, wd[:, base : base + CHUNK], preferred_element_type=jnp.float32
                )
                extra[:, base : base + CHUNK] = got[MAIN:ROWS]
                halves.append(got[0:MAIN])
            pack(arrived, first, c, *halves)
        pack_extra(arrived, first)

        def send(k, carry):
            index = first + k

            @pl.when(index == 0)
            def _():
                pltpu.make_async_copy(arrived.at[0], returned.at[0], back_recv_sem.at[0]).start()

            @pl.when(index > 0)
            def _():
                pltpu.make_async_remote_copy(
                    src_ref=arrived.at[index],
                    dst_ref=returned.at[index],
                    send_sem=back_send_sem,
                    recv_sem=back_recv_sem.at[g],
                    device_id=device(*route_source(index)),
                    device_id_type=MESH,
                ).start()

            return carry

        return lax.fori_loop(0, PER_GROUP, send, carry)

    lax.fori_loop(0, GROUPS, expert, 0)
    acc[...] = hidden[...]

    def combine(g, carry):
        first = g * PER_GROUP
        block = returned.at[pl.ds(first, PER_GROUP)]
        pltpu.make_async_copy(block, block, back_recv_sem.at[g]).wait()
        unpack(returned, first)
        gate = gates[g]
        high = gate.astype(jnp.bfloat16)
        low = (gate - high.astype(jnp.float32)).astype(jnp.bfloat16)
        both = jnp.concatenate([high, low], axis=0)
        for c in range(0, D, CHUNK):
            got = jnp.dot(both, rows[:, c : c + CHUNK], preferred_element_type=jnp.float32)
            acc[:, c : c + CHUNK] += got[0:128] + got[128:256]
        return carry

    lax.fori_loop(0, GROUPS, combine, 0)
    out[...] = acc[...].astype(jnp.bfloat16)
    sent = outbound.at[pl.ds(1, DEVICES - 1)]
    pltpu.make_async_copy(sent, sent, send_sem).wait()
    sent = arrived.at[pl.ds(1, DEVICES - 1)]
    pltpu.make_async_copy(sent, sent, back_send_sem).wait()


def routed_layer(normed, hidden, expert_ids, gate_values, w_gate, w_up, w_down):
    tokens = normed.shape[0]
    ty, tx, tc, tz = route_target(jnp.arange(DEVICES, dtype=jnp.int32))
    target = ((ty * 4 + tx) * 2 + tc) * 4 + tz
    hit = (expert_ids.T[None, :, :] == target[:, None, None])
    member = jnp.any(hit, axis=1)
    gate = jnp.sum(jnp.where(hit, gate_values.T[None, :, :], 0.0), axis=1)
    before = jnp.triu(jnp.ones((tokens, tokens), jnp.bfloat16), 1)
    position = jnp.dot(member.astype(jnp.bfloat16), before, preferred_element_type=jnp.float32)
    position = jnp.where(member, position, -1.0)
    slot = position[:, None, :] == jnp.arange(CAP, dtype=jnp.float32)[None, :, None]

    def grouped(x):
        x = x.reshape(GROUPS, PER_GROUP, CAP, tokens)
        main = x[:, :, :8].reshape(GROUPS, MAIN, tokens)
        return jnp.concatenate([main, x[:, :, 8]], axis=1)

    picks = grouped(slot.astype(jnp.bfloat16))
    gates = jnp.swapaxes(grouped(jnp.where(slot, gate[:, None, :], 0.0)), 1, 2)
    line = jnp.arange(16 * PER_GROUP, dtype=jnp.int32)
    origin = (line % PER_GROUP) * 16 + line // PER_GROUP
    perm = (origin[:, None] == line[None, :]).astype(jnp.bfloat16)
    perm_t = (line[:, None] == origin[None, :]).astype(jnp.bfloat16)
    vmem = pl.BlockSpec(memory_space=pltpu.VMEM)
    anywhere = pl.BlockSpec(memory_space=pl.ANY)
    return pl.pallas_call(
        moe_kernel,
        out_shape=jax.ShapeDtypeStruct((tokens, D), jnp.bfloat16),
        in_specs=[vmem] * 6 + [anywhere] * 3,
        out_specs=vmem,
        scratch_shapes=[
            pltpu.VMEM((DEVICES, 16, MESSAGE), jnp.bfloat16),
            pltpu.VMEM((DEVICES, 16, MESSAGE), jnp.bfloat16),
            pltpu.VMEM((DEVICES, 16, MESSAGE), jnp.bfloat16),
            pltpu.VMEM((D, FFH), jnp.bfloat16),
            pltpu.VMEM((D, FFH), jnp.bfloat16),
            pltpu.VMEM((FFH, D), jnp.bfloat16),
            pltpu.VMEM((ROWS, D), jnp.bfloat16),
            pltpu.VMEM((PER_GROUP, D), jnp.float32),
            pltpu.VMEM((tokens, D), jnp.float32),
            pltpu.SemaphoreType.DMA((3,)),
            pltpu.SemaphoreType.DMA,
            pltpu.SemaphoreType.DMA((GROUPS,)),
            pltpu.SemaphoreType.DMA,
            pltpu.SemaphoreType.DMA((GROUPS,)),
        ],
        compiler_params=pltpu.CompilerParams(
            has_side_effects=True, vmem_limit_bytes=63 * 1024 * 1024
        ),
        cost_estimate=pl.CostEstimate(
            flops=24 * 10**9, bytes_accessed=40 * 10**6, transcendentals=10**6
        ),
    )(normed, hidden, picks, gates, perm, perm_t, w_gate, w_up, w_down)


def passed_along(x, axis, by):
    count = lax.axis_size(axis)
    pairs = [(i, i + by) for i in range(count) if 0 <= i + by < count]
    return lax.ppermute(x, axis, pairs)


def doc_index(positions, doc_ends):
    return jnp.sum((positions[:, None] >= doc_ends[None, :]).astype(jnp.int32), axis=1)


def body(
    queries,
    keys,
    values,
    doc_lengths,
    out_weight,
    residual,
    norm_gain,
    expert_ids,
    gate_values,
    w_gate,
    w_up,
    w_down,
):
    row_count = queries.shape[0]
    kv_local = keys.shape[1] // HEAD_DIM
    group = queries.shape[1] // keys.shape[1]
    scale = HEAD_DIM ** (-0.5)
    doc_ends = jnp.cumsum(doc_lengths)
    my_start = lax.axis_index("seq") * row_count
    query_pos = my_start + jnp.arange(row_count, dtype=jnp.int32)
    query_doc = doc_index(query_pos, doc_ends)
    query_heads = queries.reshape(row_count, kv_local, group, HEAD_DIM)

    def attend_part(running, key_part, value_part, first):
        width = key_part.shape[0]
        key_pos = first + jnp.arange(width, dtype=jnp.int32)
        key_doc = doc_index(key_pos, doc_ends)
        visible = (
            (key_pos[None, :] >= 0)
            & (key_pos[None, :] <= query_pos[:, None])
            & (key_doc[None, :] == query_doc[:, None])
        )

        def update(state):
            top_old, total_old, accum_old = state
            scores = (
                jnp.einsum(
                    "tkgd,skd->kgts",
                    query_heads,
                    key_part.reshape(width, kv_local, HEAD_DIM),
                    preferred_element_type=jnp.float32,
                )
                * scale
            )
            masked = jnp.where(visible, scores, NEG_FILL)
            top_new = jnp.maximum(top_old, jnp.max(masked, axis=-1))
            factor = jnp.exp(top_old - top_new)
            weights = jnp.where(visible, jnp.exp(masked - top_new[..., None]), 0.0)
            total_new = total_old * factor + jnp.sum(weights, axis=-1)
            added = jnp.einsum(
                "kgts,skd->kgtd",
                weights.astype(jnp.bfloat16),
                value_part.reshape(width, kv_local, HEAD_DIM),
                preferred_element_type=jnp.float32,
            )
            return (top_new, total_new, accum_old * factor[..., None] + added)

        return lax.cond(jnp.any(visible), update, lambda state: state, running)

    def absorb(running, shards, offset):
        key_all, value_all = shards
        width = key_all.shape[0]
        step_len = width

        def inner(index, state):
            begin = index * step_len
            return attend_part(state, key_all, value_all, offset + begin)

        return lax.fori_loop(0, width // step_len, inner, running)

    start_top = jnp.full((kv_local, group, row_count), NEG_FILL, jnp.float32)
    start_total = jnp.zeros((kv_local, group, row_count), jnp.float32)
    start_accum = jnp.zeros((kv_local, group, row_count, HEAD_DIM), jnp.float32)
    initial = (start_top, start_total, start_accum)
    final_state = absorb(initial, (keys, values), my_start)
    for distance in range(1, DOC_SHARDS + 1):
        earlier = passed_along((keys, values), "seq", distance)
        final_state = absorb(final_state, earlier, my_start - distance * row_count)
    top_last, total_last, accum_last = final_state
    attended = accum_last / total_last[..., None]
    attended = (
        jnp.transpose(attended, (2, 0, 1, 3))
        .reshape(row_count, kv_local * group * HEAD_DIM)
        .astype(jnp.bfloat16)
    )
    partial_terms = jnp.dot(
        attended,
        lax.all_gather(out_weight, "seq", axis=1, tiled=True),
        preferred_element_type=jnp.float32,
    )
    projected = lax.psum_scatter(
        partial_terms.astype(jnp.bfloat16), "exp", scatter_dimension=0, tiled=True
    ).astype(jnp.float32)
    hidden_state = residual.astype(jnp.float32) + projected
    variance = jnp.mean(hidden_state * hidden_state, axis=1, keepdims=True)
    normed = (hidden_state * lax.rsqrt(variance + 1e-06) * norm_gain[None, :]).astype(jnp.bfloat16)
    return routed_layer(normed, hidden_state, expert_ids, gate_values, w_gate, w_up, w_down)


def solution(mesh):
    in_specs = (
        P("seq", "exp"),
        P("seq", "exp"),
        P("seq", "exp"),
        P(),
        P("exp", "seq"),
        P(("seq", "exp"), None),
        P(),
        P(("seq", "exp"), None),
        P(("seq", "exp"), None),
        P(("seq", "exp"), None, None),
        P(("seq", "exp"), None, None),
        P(("seq", "exp"), None, None),
    )
    out_specs = P(("seq", "exp"), None)
    return jax.shard_map(body, mesh=mesh, in_specs=in_specs, out_specs=out_specs, check_vma=False)
```

```python
import functools

import jax
import jax.numpy as jnp
from jax import lax
from jax.experimental import pallas as pl
from jax.experimental.pallas import tpu as pltpu
from jax.sharding import PartitionSpec as P

HEAD_DIM = 128
SHARD = 512
BACK = 2048
NEG_FILL = -1e30
D = 4096
HALF = D // 2
FFH = 768
CAP = 9
DEVICES = 128
GROUPS = 4
PER_GROUP = DEVICES // GROUPS
MAIN = PER_GROUP * 8
ROWS = PER_GROUP * CAP
EXTRA = D // 16
MESSAGE = HALF + EXTRA
CHUNK = 512
STRIDE = 37
MESH = pl.DeviceIdType.MESH


def place():
    seq = lax.axis_index("seq")
    return seq // 8, (seq // 2) % 4, seq % 2, lax.axis_index("exp")


def route_target(index):
    y, x, c, z = place()
    j = (index * STRIDE) % DEVICES
    dy, dx, dc, dz = j // 32, (j // 8) % 4, (j // 4) % 2, j % 4
    ey = jnp.where(c == 0, dy, dx)
    ex = jnp.where(c == 0, dx, dz)
    ez = jnp.where(c == 0, dz, dy)
    return (y + ey) % 4, (x + ex) % 4, (c + dc) % 2, (z + ez) % 4


def route_source(index):
    y, x, c, z = place()
    j = (index * STRIDE) % DEVICES
    dy, dx, dc, dz = j // 32, (j // 8) % 4, (j // 4) % 2, j % 4
    sc = (c + dc) % 2
    ey = jnp.where(sc == 0, dy, dx)
    ex = jnp.where(sc == 0, dx, dz)
    ez = jnp.where(sc == 0, dz, dy)
    return (y - ey + 4) % 4, (x - ex + 4) % 4, sc, (z - ez + 4) % 4


def device(y, x, c, z):
    return {"seq": (y * 4 + x) * 2 + c, "exp": z}


def moe_kernel(
    normed, hidden, picks, gates, perm, perm_t, w_gate, w_up, w_down, out,
    outbound, arrived, returned, wg, wu, wd, rows, extra, acc,
    weight_sem, send_sem, recv_sem, back_send_sem, back_recv_sem,
):
    loads = [
        pltpu.make_async_copy(src.at[0], dst, weight_sem.at[k])
        for k, (src, dst) in enumerate(((w_gate, wg), (w_up, wu), (w_down, wd)))
    ]
    for load in loads:
        load.start()

    def pack(buffer, first, c, left, right):
        both = jnp.concatenate(
            [left.reshape(PER_GROUP, 8, CHUNK), right.reshape(PER_GROUP, 8, CHUNK)], axis=1
        )
        buffer[pl.ds(first, PER_GROUP), :, c : c + CHUNK] = both.astype(jnp.bfloat16)

    def pack_extra(buffer, first):
        stacked = jnp.concatenate(
            [extra[:, j * EXTRA : (j + 1) * EXTRA] for j in range(16)], axis=0
        ).astype(jnp.bfloat16)
        turned = jnp.dot(perm_t[...], stacked, preferred_element_type=jnp.float32)
        buffer[pl.ds(first, PER_GROUP), :, HALF:MESSAGE] = turned.astype(jnp.bfloat16).reshape(
            PER_GROUP, 16, EXTRA
        )

    def unpack(buffer, first):
        for c in range(0, HALF, CHUNK):
            both = buffer[pl.ds(first, PER_GROUP), :, c : c + CHUNK].astype(jnp.float32)
            rows[0:MAIN, c : c + CHUNK] = both[:, 0:8].reshape(MAIN, CHUNK).astype(jnp.bfloat16)
            rows[0:MAIN, HALF + c : HALF + c + CHUNK] = (
                both[:, 8:16].reshape(MAIN, CHUNK).astype(jnp.bfloat16)
            )
        stacked = buffer[pl.ds(first, PER_GROUP), :, HALF:MESSAGE].reshape(PER_GROUP * 16, EXTRA)
        turned = jnp.dot(perm[...], stacked, preferred_element_type=jnp.float32)
        for j in range(16):
            rows[MAIN:ROWS, j * EXTRA : (j + 1) * EXTRA] = turned[
                j * PER_GROUP : (j + 1) * PER_GROUP
            ].astype(jnp.bfloat16)

    def build(g, carry):
        first = g * PER_GROUP
        for c in range(0, HALF, CHUNK):
            halves = []
            for base in (c, HALF + c):
                got = jnp.dot(
                    picks[g], normed[:, base : base + CHUNK], preferred_element_type=jnp.float32
                )
                extra[:, base : base + CHUNK] = got[MAIN:ROWS]
                halves.append(got[0:MAIN])
            pack(outbound, first, c, *halves)
        pack_extra(outbound, first)

        def send(k, carry):
            index = first + k

            @pl.when(index == 0)
            def _():
                pltpu.make_async_copy(outbound.at[0], arrived.at[0], recv_sem.at[0]).start()

            @pl.when(index > 0)
            def _():
                pltpu.make_async_remote_copy(
                    src_ref=outbound.at[index],
                    dst_ref=arrived.at[index],
                    send_sem=send_sem,
                    recv_sem=recv_sem.at[g],
                    device_id=device(*route_target(index)),
                    device_id_type=MESH,
                ).start()

            return carry

        return lax.fori_loop(0, PER_GROUP, send, carry)

    lax.fori_loop(0, GROUPS, build, 0)
    for load in loads:
        load.wait()

    def expert(g, carry):
        first = g * PER_GROUP
        block = arrived.at[pl.ds(first, PER_GROUP)]
        pltpu.make_async_copy(block, block, recv_sem.at[g]).wait()
        unpack(arrived, first)
        gate_part = jnp.dot(rows[...], wg[...], preferred_element_type=jnp.float32)
        up_part = jnp.dot(rows[...], wu[...], preferred_element_type=jnp.float32)
        inner = (gate_part / (1.0 + jnp.exp(-gate_part)) * up_part).astype(jnp.bfloat16)
        for c in range(0, HALF, CHUNK):
            halves = []
            for base in (c, HALF + c):
                got = jnp.dot(
                    inner, wd[:, base : base + CHUNK], preferred_element_type=jnp.float32
                )
                extra[:, base : base + CHUNK] = got[MAIN:ROWS]
                halves.append(got[0:MAIN])
            pack(arrived, first, c, *halves)
        pack_extra(arrived, first)

        def send(k, carry):
            index = first + k

            @pl.when(index == 0)
            def _():
                pltpu.make_async_copy(arrived.at[0], returned.at[0], back_recv_sem.at[0]).start()

            @pl.when(index > 0)
            def _():
                pltpu.make_async_remote_copy(
                    src_ref=arrived.at[index],
                    dst_ref=returned.at[index],
                    send_sem=back_send_sem,
                    recv_sem=back_recv_sem.at[g],
                    device_id=device(*route_source(index)),
                    device_id_type=MESH,
                ).start()

            return carry

        return lax.fori_loop(0, PER_GROUP, send, carry)

    lax.fori_loop(0, GROUPS, expert, 0)
    acc[...] = hidden[...]

    def combine(g, carry):
        first = g * PER_GROUP
        block = returned.at[pl.ds(first, PER_GROUP)]
        pltpu.make_async_copy(block, block, back_recv_sem.at[g]).wait()
        unpack(returned, first)
        gate = gates[g]
        high = gate.astype(jnp.bfloat16)
        low = (gate - high.astype(jnp.float32)).astype(jnp.bfloat16)
        both = jnp.concatenate([high, low], axis=0)
        for c in range(0, D, CHUNK):
            got = jnp.dot(both, rows[:, c : c + CHUNK], preferred_element_type=jnp.float32)
            acc[:, c : c + CHUNK] += got[0:128] + got[128:256]
        return carry

    lax.fori_loop(0, GROUPS, combine, 0)
    out[...] = acc[...].astype(jnp.bfloat16)
    sent = outbound.at[pl.ds(1, DEVICES - 1)]
    pltpu.make_async_copy(sent, sent, send_sem).wait()
    sent = arrived.at[pl.ds(1, DEVICES - 1)]
    pltpu.make_async_copy(sent, sent, back_send_sem).wait()


def routed_layer(normed, hidden, expert_ids, gate_values, w_gate, w_up, w_down):
    tokens = normed.shape[0]
    ty, tx, tc, tz = route_target(jnp.arange(DEVICES, dtype=jnp.int32))
    target = ((ty * 4 + tx) * 2 + tc) * 4 + tz
    hit = (expert_ids.T[None, :, :] == target[:, None, None])
    member = jnp.any(hit, axis=1)
    gate = jnp.sum(jnp.where(hit, gate_values.T[None, :, :], 0.0), axis=1)
    before = jnp.triu(jnp.ones((tokens, tokens), jnp.bfloat16), 1)
    position = jnp.dot(member.astype(jnp.bfloat16), before, preferred_element_type=jnp.float32)
    position = jnp.where(member, position, -1.0)
    slot = position[:, None, :] == jnp.arange(CAP, dtype=jnp.float32)[None, :, None]

    def grouped(x):
        x = x.reshape(GROUPS, PER_GROUP, CAP, tokens)
        main = x[:, :, :8].reshape(GROUPS, MAIN, tokens)
        return jnp.concatenate([main, x[:, :, 8]], axis=1)

    picks = grouped(slot.astype(jnp.bfloat16))
    gates = jnp.swapaxes(grouped(jnp.where(slot, gate[:, None, :], 0.0)), 1, 2)
    line = jnp.arange(16 * PER_GROUP, dtype=jnp.int32)
    origin = (line % PER_GROUP) * 16 + line // PER_GROUP
    perm = (origin[:, None] == line[None, :]).astype(jnp.bfloat16)
    perm_t = (line[:, None] == origin[None, :]).astype(jnp.bfloat16)
    vmem = pl.BlockSpec(memory_space=pltpu.VMEM)
    anywhere = pl.BlockSpec(memory_space=pl.ANY)
    return pl.pallas_call(
        moe_kernel,
        out_shape=jax.ShapeDtypeStruct((tokens, D), jnp.bfloat16),
        in_specs=[vmem] * 6 + [anywhere] * 3,
        out_specs=vmem,
        scratch_shapes=[
            pltpu.VMEM((DEVICES, 16, MESSAGE), jnp.bfloat16),
            pltpu.VMEM((DEVICES, 16, MESSAGE), jnp.bfloat16),
            pltpu.VMEM((DEVICES, 16, MESSAGE), jnp.bfloat16),
            pltpu.VMEM((D, FFH), jnp.bfloat16),
            pltpu.VMEM((D, FFH), jnp.bfloat16),
            pltpu.VMEM((FFH, D), jnp.bfloat16),
            pltpu.VMEM((ROWS, D), jnp.bfloat16),
            pltpu.VMEM((PER_GROUP, D), jnp.float32),
            pltpu.VMEM((tokens, D), jnp.float32),
            pltpu.SemaphoreType.DMA((3,)),
            pltpu.SemaphoreType.DMA,
            pltpu.SemaphoreType.DMA((GROUPS,)),
            pltpu.SemaphoreType.DMA,
            pltpu.SemaphoreType.DMA((GROUPS,)),
        ],
        compiler_params=pltpu.CompilerParams(
            has_side_effects=True, vmem_limit_bytes=63 * 1024 * 1024
        ),
        cost_estimate=pl.CostEstimate(
            flops=24 * 10**9, bytes_accessed=40 * 10**6, transcendentals=10**6
        ),
    )(normed, hidden, picks, gates, perm, perm_t, w_gate, w_up, w_down)


def rotated(chip, by):
    return (chip + by + 16) % 16


def chip_device(chip, c, z):
    return device(chip // 4, chip % 4, c, z)


def remote(src, dst, send_sem, recv_sem, target):
    return pltpu.make_async_remote_copy(
        src_ref=src, dst_ref=dst, send_sem=send_sem, recv_sem=recv_sem,
        device_id=target, device_id_type=MESH,
    )


def wait_bytes(ref, sem):
    pltpu.make_async_copy(ref, ref, sem).wait()


def front_kernel(
    doc_lengths, queries, keys, values, out_weight, residual, gain, normed, hidden,
    kv, weight, att, relay, stage, fin,
    kv_send, kv_recv, line_recv, line_fwd, plane_recv, plane_fwd, weight_send,
    att_send, att_recv, relay_recv, fin_recv, term_send,
):
    y, x, c, z = place()
    chip = y * 4 + x
    partner = device(y, x, 1 - c, z)

    def kv_slot(slot):
        return kv.at[pl.ds(pl.multiple_of(slot * SHARD, SHARD), SHARD)]

    own = pl.ds(pl.multiple_of((4 + c) * SHARD, SHARD), SHARD)
    kv[own, 0:HEAD_DIM] = keys[...]
    kv[own, HEAD_DIM : 2 * HEAD_DIM] = values[...]
    for ahead in (1, 2):
        remote(
            kv_slot(4 + c), kv_slot(4 - 2 * ahead + c), kv_send, kv_recv.at[ahead - 1],
            chip_device(rotated(chip, ahead), c, z),
        ).start()

    def spot(half, u, v):
        return 4 * v + u if half == 0 else 4 * u + v

    def spot_device(half, u, v):
        return device(v, u, c, z) if half == 0 else device(u, v, c, z)

    def cut(half, first, count, k, width=1):
        lanes = pl.ds(pl.multiple_of(k * HEAD_DIM, HEAD_DIM), width * HEAD_DIM)
        return weight.at[pl.ds(half * 512 + first, count), lanes]

    home = ((x, y), (y, x))
    weight[:, pl.ds(pl.multiple_of(chip * HEAD_DIM, HEAD_DIM), HEAD_DIM)] = out_weight[...]

    def spread(half, u):
        v = home[half][1]
        block = cut(half, 0, 512, spot(half, u, v))
        for way, step in enumerate((1, 3)):
            remote(
                block, block, weight_send, plane_recv.at[half, way],
                spot_device(half, home[half][0], (v + step) % 4),
            ).start()

    for half in (0, 1):
        u, v = home[half]
        block = cut(half, 0, 512, spot(half, u, v))
        for way, step in enumerate((1, 3)):
            remote(
                block, block, weight_send, line_recv.at[half, way],
                spot_device(half, (u + step) % 4, v),
            ).start()
    for half in (0, 1):
        spread(half, home[half][0])

    def line_step():
        for half in (0, 1):
            u, v = home[half]
            for way, step in enumerate((1, 3)):
                wait_bytes(cut(half, 0, 512, 0), line_recv.at[half, way])
                came = (u - step + 4) % 4
                part = cut(half, 256 * way, 256, spot(half, came, v))
                remote(
                    part, part, weight_send, line_fwd.at[half, way],
                    spot_device(half, (u + step) % 4, v),
                ).start()
                spread(half, came)

    def line_end():
        for half in (0, 1):
            for way in (0, 1):
                wait_bytes(cut(half, 0, 256, 0), line_fwd.at[half, way])
            spread(half, (home[half][0] + 2) % 4)

    def plane_step():
        for half in (0, 1):
            u, v = home[half]
            for way, step in enumerate((1, 3)):
                wait_bytes(cut(half, 0, 512, 0, 4), plane_recv.at[half, way])
                came = (v - step + 4) % 4
                target = spot_device(half, u, (v + step) % 4)
                if half == 0:
                    parts = [cut(half, 256 * way, 256, 4 * came, 4)]
                else:
                    parts = [cut(half, 256 * way, 256, spot(half, i, came)) for i in range(4)]
                for part in parts:
                    remote(part, part, weight_send, plane_fwd.at[half, way], target).start()

    def plane_end():
        for half in (0, 1):
            for way in (0, 1):
                wait_bytes(cut(half, 0, 256, 0, 4), plane_fwd.at[half, way])

    for k in (0, 1):
        wait_bytes(kv_slot(0), kv_recv.at[k])
    for k, slot in enumerate((jnp.where(c == 0, 4, 1), 2 + c)):
        remote(kv_slot(slot), kv_slot(slot), kv_send, kv_recv.at[2 + k], partner).start()
    line_step()
    for k in (2, 3):
        wait_bytes(kv_slot(0), kv_recv.at[k])

    ends = []
    total_len = doc_lengths[0]
    for i in range(doc_lengths.shape[0]):
        if i:
            total_len = total_len + doc_lengths[i]
        ends.append(total_len)
    factor = HEAD_DIM ** (-0.5) * 1.4426950408889634

    def attend(b, carry):
        base = pl.multiple_of(512 * c + 128 * b, 128)
        first = (chip * 2 + c) * SHARD + b * 128
        pos = first + lax.broadcasted_iota(jnp.int32, (128, 1), 0)
        low = jnp.zeros((128, 1), jnp.int32)
        for end in ends:
            low = jnp.where(pos >= end, end, low)
        low = low - (first - BACK)
        low = jnp.concatenate([low, low], axis=0)

        def heads(hp, carry):
            lanes = pl.multiple_of(hp * 256, 256)
            both = queries[pl.ds(pl.multiple_of(b * 128, 128), 128), pl.ds(lanes, 256)]
            q = jnp.concatenate([both[:, 0:128], both[:, 128:256]], axis=0)
            nt = (((1,), (1,)), ((), ()))
            far = lax.dot_general(
                q, kv[pl.ds(base, BACK), 0:HEAD_DIM], nt, preferred_element_type=jnp.float32
            )
            near = lax.dot_general(
                q, kv[pl.ds(base + BACK, 128), 0:HEAD_DIM], nt,
                preferred_element_type=jnp.float32,
            )
            at = lax.broadcasted_iota(jnp.int32, (256, BACK), 1)
            far = jnp.where(at >= low, far, NEG_FILL)
            at = lax.broadcasted_iota(jnp.int32, (256, 128), 1)
            row = lax.broadcasted_iota(jnp.int32, (256, 128), 0) % 128
            near = jnp.where((at + BACK >= low) & (at <= row), near, NEG_FILL)
            top = jnp.maximum(
                jnp.max(far, axis=1, keepdims=True), jnp.max(near, axis=1, keepdims=True)
            )
            far = jnp.exp2((far - top) * factor)
            near = jnp.exp2((near - top) * factor)
            total = jnp.sum(far, axis=1, keepdims=True) + jnp.sum(near, axis=1, keepdims=True)
            got = jnp.dot(
                far.astype(jnp.bfloat16), kv[pl.ds(base, BACK), HEAD_DIM : 2 * HEAD_DIM],
                preferred_element_type=jnp.float32,
            ) + jnp.dot(
                near.astype(jnp.bfloat16),
                kv[pl.ds(base + BACK, 128), HEAD_DIM : 2 * HEAD_DIM],
                preferred_element_type=jnp.float32,
            )
            got = (got / total).astype(jnp.bfloat16)
            att[b, c, :, pl.ds(lanes, 256)] = jnp.concatenate([got[0:128], got[128:256]], axis=1)
            return carry

        lax.fori_loop(0, 4, heads, 0)
        remote(att.at[b, c], att.at[b, c], att_send, att_recv, partner).start()
        pl.when(b == 0)(line_end)
        pl.when(b == 2)(plane_step)
        return carry

    lax.fori_loop(0, 4, attend, 0)
    plane_end()
    wait_bytes(stage.at[pl.ds(0, 4)], att_recv)

    def terms(tz, half):
        return jnp.dot(
            att[tz].reshape(256, 1024), weight[:, half * 1024 : (half + 1) * 1024],
            preferred_element_type=jnp.float32,
        )

    def put(step, half, value):
        at = (step * 2 + half) * 2
        stage[at : at + 2] = value.astype(jnp.bfloat16).reshape(2, 128, 1024)
        return at

    up, down = (z + 1) % 4, (z + 3) % 4
    far_z = (z + 2) % 4
    for half, nearer in enumerate((up, down)):
        at = put(0, half, terms(far_z, half))
        remote(
            stage.at[pl.ds(at, 2)], relay.at[half], term_send, relay_recv.at[half],
            device(y, x, c, nearer),
        ).start()

    def deliver(side, half, tz, at):
        for tc in (0, 1):
            remote(
                stage.at[at + tc], fin.at[(side * 2 + c) * 2 + half], term_send, fin_recv,
                device(y, x, tc, tz),
            ).start()

    deliver(0, 1, up, put(1, 1, terms(up, 1)))
    deliver(1, 0, down, put(2, 0, terms(down, 0)))
    for half in (0, 1):
        at = put(3, half, terms(z, half))
        spot_at = (2 * 2 + c) * 2 + half
        fin[spot_at] = stage[at + c]
        remote(stage.at[at + 1 - c], fin.at[spot_at], term_send, fin_recv, partner).start()
    for half, tz in enumerate((up, down)):
        value = terms(tz, half)
        wait_bytes(relay.at[half], relay_recv.at[half])
        value = value + relay[half].reshape(256, 1024).astype(jnp.float32)
        deliver(half, half, tz, put(1 + half, half, value))

    wait_bytes(fin.at[pl.ds(0, 10)], fin_recv)
    squares = jnp.zeros((128, HEAD_DIM), jnp.float32)
    for cs in (0, 1):
        for k in range(16):
            half, kk = k // 8, k % 8
            lanes = slice((2 * k + cs) * 128, (2 * k + cs + 1) * 128)
            value = residual[:, lanes].astype(jnp.float32)
            for side in range(3):
                value = value + fin[
                    (side * 2 + cs) * 2 + half, :, kk * 128 : (kk + 1) * 128
                ].astype(jnp.float32)
            hidden[:, lanes] = value
            squares = squares + value * value
    variance = jnp.sum(squares, axis=1, keepdims=True) * (1.0 / D)
    shrink = lax.rsqrt(variance + 1e-06)
    for first in range(0, D, CHUNK):
        lanes = slice(first, first + CHUNK)
        normed[:, lanes] = (hidden[:, lanes] * shrink * gain[:, lanes]).astype(jnp.bfloat16)

    for _ in range(4):
        wait_bytes(kv_slot(0), kv_send)
    wait_bytes(weight.at[:, 0:1920], weight_send)
    wait_bytes(stage.at[pl.ds(0, 4)], att_send)
    wait_bytes(stage.at[pl.ds(0, 14)], term_send)


def front(queries, keys, values, doc_lengths, out_weight, residual, norm_gain):
    vmem = pl.BlockSpec(memory_space=pltpu.VMEM)
    dma = pltpu.SemaphoreType.DMA
    tokens = residual.shape[0]
    return pl.pallas_call(
        front_kernel,
        out_shape=(
            jax.ShapeDtypeStruct((tokens, D), jnp.bfloat16),
            jax.ShapeDtypeStruct((tokens, D), jnp.float32),
        ),
        in_specs=[pl.BlockSpec(memory_space=pltpu.SMEM)] + [vmem] * 6,
        out_specs=(vmem, vmem),
        scratch_shapes=[
            pltpu.VMEM((6 * SHARD, 2 * HEAD_DIM), jnp.bfloat16),
            pltpu.VMEM((1024, HALF), jnp.bfloat16),
            pltpu.VMEM((4, 2, 128, 1024), jnp.bfloat16),
            pltpu.VMEM((2, 2, 128, 1024), jnp.bfloat16),
            pltpu.VMEM((16, 128, 1024), jnp.bfloat16),
            pltpu.VMEM((12, 128, 1024), jnp.bfloat16),
            dma, dma((4,)), dma((2, 2)), dma((2, 2)), dma((2, 2)), dma((2, 2)), dma,
            dma, dma, dma((2,)), dma, dma,
        ],
        compiler_params=pltpu.CompilerParams(
            has_side_effects=True, vmem_limit_bytes=60 * 1024 * 1024
        ),
        cost_estimate=pl.CostEstimate(
            flops=10**10, bytes_accessed=10**7, transcendentals=10**7
        ),
    )(doc_lengths, queries, keys, values, out_weight, residual, norm_gain.reshape(1, D))


def body(
    queries, keys, values, doc_lengths, out_weight, residual, norm_gain, expert_ids,
    gate_values, w_gate, w_up, w_down,
):
    normed, hidden = front(queries, keys, values, doc_lengths, out_weight, residual, norm_gain)
    return routed_layer(normed, hidden, expert_ids, gate_values, w_gate, w_up, w_down)


def solution(mesh):
    in_specs = (
        P("seq", "exp"),
        P("seq", "exp"),
        P("seq", "exp"),
        P(),
        P("exp", "seq"),
        P(("seq", "exp"), None),
        P(),
        P(("seq", "exp"), None),
        P(("seq", "exp"), None),
        P(("seq", "exp"), None, None),
        P(("seq", "exp"), None, None),
        P(("seq", "exp"), None, None),
    )
    out_specs = P(("seq", "exp"), None)
    return jax.shard_map(body, mesh=mesh, in_specs=in_specs, out_specs=out_specs, check_vma=False)
```

```python
import functools

import jax
import jax.numpy as jnp
from jax import lax
from jax.experimental import pallas as pl
from jax.experimental.pallas import tpu as pltpu
from jax.sharding import PartitionSpec as P

HEAD_DIM = 128
SHARD = 512
NEG_FILL = -1e30
D = 4096
HALF = D // 2
FFH = 768
CAP = 9
TOPK = 8
DEVICES = 128
GROUPS = 4
PER_GROUP = DEVICES // GROUPS
MAIN = PER_GROUP * 8
ROWS = PER_GROUP * CAP
EXTRA = D // 16
MESSAGE = HALF + EXTRA
CHUNK = 512
STRIDE = 37
MESH = pl.DeviceIdType.MESH


def place():
    seq = lax.axis_index("seq")
    return seq // 8, (seq // 2) % 4, seq % 2, lax.axis_index("exp")


def device(y, x, c, z):
    return {"seq": (y * 4 + x) * 2 + c, "exp": z}


def route_target(index):
    y, x, c, z = place()
    j = (index * STRIDE) % DEVICES
    dy, dx, dc, dz = j // 32, (j // 8) % 4, (j // 4) % 2, j % 4
    ey = jnp.where(c == 0, dy, dx)
    ex = jnp.where(c == 0, dx, dz)
    ez = jnp.where(c == 0, dz, dy)
    return (y + ey) % 4, (x + ex) % 4, (c + dc) % 2, (z + ez) % 4


def route_source(index):
    y, x, c, z = place()
    j = (index * STRIDE) % DEVICES
    dy, dx, dc, dz = j // 32, (j // 8) % 4, (j // 4) % 2, j % 4
    sc = (c + dc) % 2
    ey = jnp.where(sc == 0, dy, dx)
    ex = jnp.where(sc == 0, dx, dz)
    ez = jnp.where(sc == 0, dz, dy)
    return (y - ey + 4) % 4, (x - ex + 4) % 4, sc, (z - ez + 4) % 4


def target_ids(first):
    y, x, c, z = place()
    index = first + lax.broadcasted_iota(jnp.int32, (1, PER_GROUP), 1)
    j = (index * STRIDE) & (DEVICES - 1)
    dy, dx, dc, dz = j >> 5, (j >> 3) & 3, (j >> 2) & 1, j & 3
    ey = jnp.where(c == 0, dy, dx)
    ex = jnp.where(c == 0, dx, dz)
    ez = jnp.where(c == 0, dz, dy)
    ty, tx, tc, tz = (y + ey) & 3, (x + ex) & 3, (c + dc) & 1, (z + ez) & 3
    return (((ty * 4 + tx) * 2 + tc) * 4 + tz).astype(jnp.float32)


def slot_of(row):
    return jnp.where(row < MAIN, row >> 3, row - MAIN), jnp.where(row < MAIN, row & 7, 8)


def moe_kernel(
    normed, hidden, ids_t, gates_t, w_gate, w_up, w_down, out,
    outbound, arrived, returned, wg, wu, wd, rows, extra, acc, perm, posn, gate,
    weight_sem, hidden_sem, send_sem, recv_sem, back_send_sem, back_recv_sem,
):
    tokens = normed.shape[0]
    loads = [
        pltpu.make_async_copy(src.at[0], dst, weight_sem.at[k])
        for k, (src, dst) in enumerate(((w_gate, wg), (w_up, wu), (w_down, wd)))
    ]
    for load in loads:
        load.start()
    fetch = pltpu.make_async_copy(hidden, acc, hidden_sem)
    fetch.start()
    line = lax.broadcasted_iota(jnp.int32, (16 * PER_GROUP, 16 * PER_GROUP), 0)
    other = lax.broadcasted_iota(jnp.int32, (16 * PER_GROUP, 16 * PER_GROUP), 1)
    perm[...] = (other == (line & (PER_GROUP - 1)) * 16 + (line >> 5)).astype(jnp.bfloat16)

    def pack(buffer, first, c, left, right):
        both = jnp.concatenate(
            [left.reshape(PER_GROUP, 8, CHUNK), right.reshape(PER_GROUP, 8, CHUNK)], axis=1
        )
        buffer[pl.ds(first, PER_GROUP), :, c : c + CHUNK] = both.astype(jnp.bfloat16)

    def pack_extra(buffer, first):
        stacked = jnp.concatenate(
            [extra[:, j * EXTRA : (j + 1) * EXTRA] for j in range(16)], axis=0
        ).astype(jnp.bfloat16)
        turned = lax.dot_general(
            perm[...], stacked, (((0,), (0,)), ((), ())), preferred_element_type=jnp.float32
        )
        buffer[pl.ds(first, PER_GROUP), :, HALF:MESSAGE] = turned.astype(jnp.bfloat16).reshape(
            PER_GROUP, 16, EXTRA
        )

    def unpack(buffer, first):
        for c in range(0, HALF, CHUNK):
            both = buffer[pl.ds(first, PER_GROUP), :, c : c + CHUNK].astype(jnp.float32)
            rows[0:MAIN, c : c + CHUNK] = both[:, 0:8].reshape(MAIN, CHUNK).astype(jnp.bfloat16)
            rows[0:MAIN, HALF + c : HALF + c + CHUNK] = (
                both[:, 8:16].reshape(MAIN, CHUNK).astype(jnp.bfloat16)
            )
        stacked = buffer[pl.ds(first, PER_GROUP), :, HALF:MESSAGE].reshape(PER_GROUP * 16, EXTRA)
        turned = jnp.dot(perm[...], stacked, preferred_element_type=jnp.float32)
        for j in range(16):
            rows[MAIN:ROWS, j * EXTRA : (j + 1) * EXTRA] = turned[
                j * PER_GROUP : (j + 1) * PER_GROUP
            ].astype(jnp.bfloat16)

    routes = jnp.transpose(
        jnp.concatenate(
            [
                ids_t[...].astype(jnp.float32), gates_t[...],
                jnp.zeros((tokens - 2 * TOPK, tokens), jnp.float32),
            ],
            axis=0,
        )
    )
    earlier = (
        lax.broadcasted_iota(jnp.int32, (tokens, tokens), 0)
        > lax.broadcasted_iota(jnp.int32, (tokens, tokens), 1)
    ).astype(jnp.bfloat16)

    def build(q, carry):
        first = q * PER_GROUP
        target = target_ids(first)
        member = jnp.zeros((tokens, PER_GROUP), jnp.float32)
        weight = jnp.zeros((tokens, PER_GROUP), jnp.float32)
        for k in range(TOPK):
            hit = routes[:, k : k + 1] == target
            member = jnp.where(hit, 1.0, member)
            weight = jnp.where(hit, routes[:, TOPK + k : TOPK + k + 1], weight)
        count = jnp.dot(earlier, member.astype(jnp.bfloat16), preferred_element_type=jnp.float32)
        count = jnp.where(member > 0.0, count, -1.0)
        posn[q] = count
        gate[q] = weight
        row = lax.broadcasted_iota(jnp.int32, (ROWS, PER_GROUP), 0)
        message, _ = slot_of(row)
        spread = (message == lax.broadcasted_iota(jnp.int32, (ROWS, PER_GROUP), 1)).astype(
            jnp.bfloat16
        )
        picked = lax.dot_general(
            spread, count.astype(jnp.bfloat16), (((1,), (1,)), ((), ())),
            preferred_element_type=jnp.float32,
        )
        _, slot = slot_of(lax.broadcasted_iota(jnp.int32, (ROWS, tokens), 0))
        picks = (picked == slot.astype(jnp.float32)).astype(jnp.bfloat16)
        for c in range(0, HALF, CHUNK):
            halves = []
            for base in (c, HALF + c):
                got = jnp.dot(
                    picks, normed[:, base : base + CHUNK], preferred_element_type=jnp.float32
                )
                extra[:, base : base + CHUNK] = got[MAIN:ROWS]
                halves.append(got[0:MAIN])
            pack(outbound, first, c, *halves)
        pack_extra(outbound, first)

        def send(k, carry):
            index = first + k

            @pl.when(index == 0)
            def _():
                pltpu.make_async_copy(outbound.at[0], arrived.at[0], recv_sem.at[0]).start()

            @pl.when(index > 0)
            def _():
                pltpu.make_async_remote_copy(
                    src_ref=outbound.at[index],
                    dst_ref=arrived.at[index],
                    send_sem=send_sem,
                    recv_sem=recv_sem.at[q],
                    device_id=device(*route_target(index)),
                    device_id_type=MESH,
                ).start()

            return carry

        return lax.fori_loop(0, PER_GROUP, send, carry)

    lax.fori_loop(0, GROUPS, build, 0)
    for load in loads:
        load.wait()

    def expert(q, carry):
        first = q * PER_GROUP
        block = arrived.at[pl.ds(first, PER_GROUP)]
        pltpu.make_async_copy(block, block, recv_sem.at[q]).wait()
        unpack(arrived, first)
        gate_part = jnp.dot(rows[...], wg[...], preferred_element_type=jnp.float32)
        up_part = jnp.dot(rows[...], wu[...], preferred_element_type=jnp.float32)
        inner = (gate_part / (1.0 + jnp.exp(-gate_part)) * up_part).astype(jnp.bfloat16)
        for c in range(0, HALF, CHUNK):
            halves = []
            for base in (c, HALF + c):
                got = jnp.dot(
                    inner, wd[:, base : base + CHUNK], preferred_element_type=jnp.float32
                )
                extra[:, base : base + CHUNK] = got[MAIN:ROWS]
                halves.append(got[0:MAIN])
            pack(arrived, first, c, *halves)
        pack_extra(arrived, first)

        def send(k, carry):
            index = first + k

            @pl.when(index == 0)
            def _():
                pltpu.make_async_copy(arrived.at[0], returned.at[0], back_recv_sem.at[0]).start()

            @pl.when(index > 0)
            def _():
                pltpu.make_async_remote_copy(
                    src_ref=arrived.at[index],
                    dst_ref=returned.at[index],
                    send_sem=back_send_sem,
                    recv_sem=back_recv_sem.at[q],
                    device_id=device(*route_source(index)),
                    device_id_type=MESH,
                ).start()

            return carry

        return lax.fori_loop(0, PER_GROUP, send, carry)

    lax.fori_loop(0, GROUPS, expert, 0)
    row = lax.broadcasted_iota(jnp.int32, (PER_GROUP, ROWS), 1)
    message, _ = slot_of(row)
    gather = (message == lax.broadcasted_iota(jnp.int32, (PER_GROUP, ROWS), 0)).astype(jnp.bfloat16)
    _, slot = slot_of(lax.broadcasted_iota(jnp.int32, (tokens, ROWS), 1))
    slot = slot.astype(jnp.float32)

    def combine(q, carry):
        first = q * PER_GROUP
        block = returned.at[pl.ds(first, PER_GROUP)]
        pltpu.make_async_copy(block, block, back_recv_sem.at[q]).wait()
        unpack(returned, first)
        spread = functools.partial(jnp.dot, preferred_element_type=jnp.float32)
        used = spread(posn[q].astype(jnp.bfloat16), gather) == slot
        high = gate[q].astype(jnp.bfloat16)
        low = (gate[q] - high.astype(jnp.float32)).astype(jnp.bfloat16)
        both = jnp.concatenate(
            [jnp.where(used, spread(half, gather), 0.0) for half in (high, low)], axis=0
        ).astype(jnp.bfloat16)
        for c in range(0, D, CHUNK):
            got = jnp.dot(both, rows[:, c : c + CHUNK], preferred_element_type=jnp.float32)
            acc[:, c : c + CHUNK] += got[0:tokens] + got[tokens : 2 * tokens]
        return carry

    fetch.wait()
    lax.fori_loop(0, GROUPS, combine, 0)
    out[...] = acc[...].astype(jnp.bfloat16)
    sent = outbound.at[pl.ds(1, DEVICES - 1)]
    for sem in (send_sem, back_send_sem):
        pltpu.make_async_copy(sent, sent, sem).wait()


def routed_layer(normed, hidden, expert_ids, gate_values, w_gate, w_up, w_down):
    tokens = normed.shape[0]
    vmem = pl.BlockSpec(memory_space=pltpu.VMEM)
    anywhere = pl.BlockSpec(memory_space=pl.ANY)
    dma = pltpu.SemaphoreType.DMA
    messages = pltpu.VMEM((DEVICES, 16, MESSAGE), jnp.bfloat16)
    return pl.pallas_call(
        moe_kernel,
        out_shape=jax.ShapeDtypeStruct((tokens, D), jnp.bfloat16),
        in_specs=[vmem, anywhere, vmem, vmem] + [anywhere] * 3,
        out_specs=vmem,
        scratch_shapes=[
            messages, messages, messages,
            pltpu.VMEM((D, FFH), jnp.bfloat16),
            pltpu.VMEM((D, FFH), jnp.bfloat16),
            pltpu.VMEM((FFH, D), jnp.bfloat16),
            pltpu.VMEM((ROWS, D), jnp.bfloat16),
            pltpu.VMEM((PER_GROUP, D), jnp.float32),
            pltpu.VMEM((tokens, D), jnp.float32),
            pltpu.VMEM((16 * PER_GROUP, 16 * PER_GROUP), jnp.bfloat16),
            pltpu.VMEM((GROUPS, tokens, PER_GROUP), jnp.float32),
            pltpu.VMEM((GROUPS, tokens, PER_GROUP), jnp.float32),
            dma((3,)), dma, dma, dma((GROUPS,)), dma, dma((GROUPS,)),
        ],
        compiler_params=pltpu.CompilerParams(
            has_side_effects=True, vmem_limit_bytes=64 * 1024 * 1024
        ),
        cost_estimate=pl.CostEstimate(
            flops=24 * 10**9, bytes_accessed=40 * 10**6, transcendentals=10**6
        ),
    )(normed, hidden, expert_ids.T, gate_values.T, w_gate, w_up, w_down)


def rotated(chip, by):
    return (chip + by) % 16


def chip_device(chip, c, z):
    return device(chip // 4, chip % 4, c, z)


def remote(src, dst, send_sem, recv_sem, target):
    return pltpu.make_async_remote_copy(
        src_ref=src, dst_ref=dst, send_sem=send_sem, recv_sem=recv_sem,
        device_id=target, device_id_type=MESH,
    )


def wait_bytes(ref, sem):
    pltpu.make_async_copy(ref, ref, sem).wait()


def front_kernel(
    doc_lengths, queries, keys, values, out_weight, residual, gain, normed, hidden,
    kv, weight, att, relay, stage, fin, tops, totals, sums,
    kv_send, kv_recv, line_recv, line_fwd, plane_recv, plane_fwd, weight_send,
    att_send, att_recv, relay_recv, fin_recv, term_send,
):
    y, x, c, z = place()
    chip = y * 4 + x
    partner = device(y, x, 1 - c, z)
    barrier = pltpu.get_barrier_semaphore()
    peers = [partner]
    for by in (1, 2, 14, 15):
        peers.append(chip_device(rotated(chip, by), c, z))
    for by in (1, 3):
        peers.append(device(y, (x + by) % 4, c, z))
        peers.append(device((y + by) % 4, x, c, z))
        peers.append(device(y, x, c, (z + by) % 4))
        peers.append(device(y, x, 1 - c, (z + by) % 4))
    for peer in peers:
        pl.semaphore_signal(barrier, inc=1, device_id=peer, device_id_type=MESH)
    pl.semaphore_wait(barrier, len(peers))

    def kv_slot(slot):
        return kv.at[pl.ds(pl.multiple_of(slot * SHARD, SHARD), SHARD)]

    weight[chip] = out_weight[...]

    def spread(u):
        block = weight.at[4 * y + u]
        for way, step in enumerate((1, 3)):
            remote(
                block, block, weight_send, plane_recv.at[way], device((y + step) % 4, x, c, z)
            ).start()

    for way, step in enumerate((1, 3)):
        block = weight.at[chip]
        remote(
            block, block, weight_send, line_recv.at[way], device(y, (x + step) % 4, c, z)
        ).start()
    spread(x)
    own = pl.ds(pl.multiple_of((4 + c) * SHARD, SHARD), SHARD)
    kv[own, 0:HEAD_DIM] = keys[...]
    kv[own, HEAD_DIM : 2 * HEAD_DIM] = values[...]
    for ahead in (1, 2):
        remote(
            kv_slot(4 + c), kv_slot(4 - 2 * ahead + c), kv_send, kv_recv.at[ahead - 1],
            chip_device(rotated(chip, ahead), c, z),
        ).start()

    def line_step():
        for way, step in enumerate((1, 3)):
            wait_bytes(weight.at[0], line_recv.at[way])
            came = (x - step + 4) % 4
            part = weight.at[4 * y + came, pl.ds(512 * way, 512)]
            remote(
                part, part, weight_send, line_fwd.at[way], device(y, (x + step) % 4, c, z)
            ).start()
            spread(came)

    def line_end():
        for way in (0, 1):
            wait_bytes(weight.at[0, pl.ds(0, 512)], line_fwd.at[way])
        spread((x + 2) % 4)

    def plane_step(way):
        step = (1, 3)[way]
        wait_bytes(weight.at[pl.ds(0, 4)], plane_recv.at[way])
        came = (y - step + 4) % 4
        part = weight.at[pl.ds(4 * came, 4), pl.ds(512 * way, 512)]
        remote(
            part, part, weight_send, plane_fwd.at[way], device((y + step) % 4, x, c, z)
        ).start()

    def plane_end():
        for way in (0, 1):
            wait_bytes(weight.at[pl.ds(0, 4), pl.ds(0, 512)], plane_fwd.at[way])

    def hand_over(slot, sem):
        remote(kv_slot(slot), kv_slot(slot), kv_send, kv_recv.at[sem], partner).start()

    pl.when(c == 0)(lambda: hand_over(4, 2))
    ends = []
    total_len = doc_lengths[0]
    for i in range(doc_lengths.shape[0]):
        if i:
            total_len = total_len + doc_lengths[i]
        ends.append(total_len)
    factor = HEAD_DIM ** (-0.5) * 1.4426950408889634

    def row_of(j):
        return (y + (0, 3, 1, 2)[j]) % 4

    def term(i, j):
        columns = [weight[4 * row_of(j) + u] for u in range(4)]
        return jnp.dot(
            att[i].reshape(256, 1024), jnp.concatenate(columns, axis=1),
            preferred_element_type=jnp.float32,
        )

    def put(i, j, value):
        at = (i * 4 + row_of(j)) * 2
        stage[pl.ds(at, 2)] = value.astype(jnp.bfloat16).reshape(2, 128, 512)
        return at

    up, down = (z + 1) % 4, (z + 3) % 4

    def deliver(i, j, value):
        at = put(i, j, value)
        for tc in (0, 1):
            remote(
                stage.at[at + tc], fin.at[((i - 1) * 2 + c) * 4 + row_of(j)], term_send, fin_recv,
                device(y, x, tc, (up, down)[i - 1]),
            ).start()

    def relay_out(j):
        at = put(0, j, term(0, j))
        remote(
            stage.at[pl.ds(at, 2)], relay.at[pl.ds(2 * row_of(j), 2)], term_send, relay_recv.at[j],
            device(y, x, c, (up, down)[j % 2]),
        ).start()

    def direct(i, j):
        deliver(i, j, term(i, j))

    def relayed(i, j):
        value = term(i, j)
        wait_bytes(relay.at[pl.ds(0, 2)], relay_recv.at[j])
        passed = relay[pl.ds(2 * row_of(j), 2)].reshape(256, 512)
        deliver(i, j, value + passed.astype(jnp.float32))

    def keep(j):
        at = put(3, j, term(3, j))
        spot = (4 + c) * 4 + row_of(j)
        fin[spot] = stage[at + c]
        remote(stage.at[at + 1 - c], fin.at[spot], term_send, fin_recv, partner).start()

    def after_far():
        wait_bytes(stage.at[pl.ds(0, 2)], att_recv.at[0])
        relay_out(0)
        plane_step(0)
        plane_step(1)
        relay_out(1)
        relay_out(2)

    def after_up():
        wait_bytes(stage.at[pl.ds(0, 2)], att_recv.at[1])
        relayed(1, 0)
        direct(1, 1)

    def after_down():
        wait_bytes(stage.at[pl.ds(0, 2)], att_recv.at[2])
        direct(2, 0)
        direct(2, 2)
        relayed(2, 1)
        relayed(1, 2)

    def after_own():
        wait_bytes(stage.at[pl.ds(0, 2)], att_recv.at[3])
        plane_end()
        relay_out(3)
        direct(1, 3)
        for j in range(4):
            keep(j)
        relayed(2, 3)

    def attend(slots, first, last):
        held = [kv_slot(slot) for slot in slots]
        starts = [(chip - 2) * 2 * SHARD + slot * SHARD for slot in slots]

        def block(i, carry):
            b = (z + jnp.where(i == 2, 3, jnp.where(i == 3, 0, 2 - i))) % 4
            pos = (chip * 2 + c) * SHARD + b * 128 + lax.broadcasted_iota(jnp.int32, (128, 1), 0)
            low = jnp.zeros((128, 1), jnp.int32)
            for end in ends:
                low = jnp.where(pos >= end, end, low)
            low = jnp.concatenate([low, low], axis=0)
            high = jnp.concatenate([pos, pos], axis=0)

            def heads(hp):
                n = i * 4 + hp
                lanes = hp * 256
                both = queries[pl.ds(pl.multiple_of(b * 128, 128), 128), pl.ds(lanes, 256)]
                q = jnp.concatenate([both[:, 0:128], both[:, 128:256]], axis=0)
                at = lax.broadcasted_iota(jnp.int32, (256, SHARD), 1)
                scores, top = [], None
                for ref, start in zip(held, starts):
                    part = lax.dot_general(
                        q, ref[:, 0:HEAD_DIM], (((1,), (1,)), ((), ())),
                        preferred_element_type=jnp.float32,
                    )
                    seen = at >= low - start
                    if first:
                        seen = seen & (at <= high - start)
                    part = jnp.where(seen, part, NEG_FILL)
                    peak = jnp.max(part, axis=1, keepdims=True)
                    top = peak if top is None else jnp.maximum(top, peak)
                    scores.append(part)
                if not first:
                    old = tops[n][:, 0:1]
                    top = jnp.maximum(top, old)
                    shrink = jnp.exp2((old - top) * factor)
                    total = totals[n][:, 0:1] * shrink
                    got = sums[n] * shrink
                for part, ref in zip(scores, held):
                    weights = jnp.exp2((part - top) * factor)
                    more = jnp.sum(weights, axis=1, keepdims=True)
                    value = jnp.dot(
                        weights.astype(jnp.bfloat16), ref[:, HEAD_DIM : 2 * HEAD_DIM],
                        preferred_element_type=jnp.float32,
                    )
                    if first:
                        total, got = more, value
                    else:
                        total, got = total + more, got + value
                if not last:
                    tops[n] = jnp.broadcast_to(top, (256, 128))
                    totals[n] = jnp.broadcast_to(total, (256, 128))
                    sums[n] = got
                else:
                    got = (got / total).astype(jnp.bfloat16)
                    att[i, c, :, pl.ds(lanes, 256)] = jnp.concatenate(
                        [got[0:128], got[128:256]], axis=1
                    )

            for hp in range(4):
                heads(hp)
                if last and hp == 1:
                    for k, then in enumerate((after_far, after_up, after_down)):
                        pl.when(i == k + 1)(then)
            if last:
                remote(att.at[i, c], att.at[i, c], att_send, att_recv.at[i], partner).start()
            return carry

        lax.fori_loop(0, 4, block, 0)

    attend([4 + c], True, False)
    line_step()
    wait_bytes(kv_slot(0), kv_recv.at[0])
    hand_over(2 + c, 3)
    wait_bytes(kv_slot(0), kv_recv.at[3])
    attend([2, 3], False, False)
    line_end()
    wait_bytes(kv_slot(0), kv_recv.at[1])
    pl.when(c == 1)(lambda: hand_over(1, 2))
    wait_bytes(kv_slot(0), kv_recv.at[2])
    attend([jnp.where(c == 0, 0, 4), 1], False, True)
    after_own()
    wait_bytes(fin.at[pl.ds(0, 20)], fin_recv)
    squares = jnp.zeros((128, HEAD_DIM), jnp.float32)
    for cs in (0, 1):
        for k in range(16):
            r, u = k // 4, k % 4
            lanes = slice((2 * k + cs) * 128, (2 * k + cs + 1) * 128)
            value = residual[:, lanes].astype(jnp.float32)
            for side in range(3):
                value = value + fin[
                    (side * 2 + cs) * 4 + r, :, u * 128 : (u + 1) * 128
                ].astype(jnp.float32)
            hidden[:, lanes] = value
            squares = squares + value * value
    variance = jnp.sum(squares, axis=1, keepdims=True) * (1.0 / D)
    shrink = lax.rsqrt(variance + 1e-06)
    for first in range(0, D, CHUNK):
        lanes = slice(first, first + CHUNK)
        normed[:, lanes] = (hidden[:, lanes] * shrink * gain[:, lanes]).astype(jnp.bfloat16)

    for _ in range(4):
        wait_bytes(kv_slot(0), kv_send)
    wait_bytes(weight.at[pl.ds(0, 15)], weight_send)
    wait_bytes(stage.at[pl.ds(0, 8)], att_send)
    wait_bytes(stage.at[pl.ds(0, 28)], term_send)


def front(queries, keys, values, doc_lengths, out_weight, residual, norm_gain):
    vmem = pl.BlockSpec(memory_space=pltpu.VMEM)
    dma = pltpu.SemaphoreType.DMA
    tokens = residual.shape[0]
    return pl.pallas_call(
        front_kernel,
        out_shape=(
            jax.ShapeDtypeStruct((tokens, D), jnp.bfloat16),
            jax.ShapeDtypeStruct((tokens, D), jnp.float32),
        ),
        in_specs=[pl.BlockSpec(memory_space=pltpu.SMEM)] + [vmem] * 6,
        out_specs=(vmem, vmem),
        scratch_shapes=[
            pltpu.VMEM((6 * SHARD, 2 * HEAD_DIM), jnp.bfloat16),
            pltpu.VMEM((16, 1024, HEAD_DIM), jnp.bfloat16),
            pltpu.VMEM((4, 2, 128, 1024), jnp.bfloat16),
            pltpu.VMEM((8, 128, 512), jnp.bfloat16),
            pltpu.VMEM((32, 128, 512), jnp.bfloat16),
            pltpu.VMEM((24, 128, 512), jnp.bfloat16),
            pltpu.VMEM((16, 256, 128), jnp.float32),
            pltpu.VMEM((16, 256, 128), jnp.float32),
            pltpu.VMEM((16, 256, 128), jnp.float32),
            dma, dma((4,)), dma((2,)), dma((2,)), dma((2,)), dma((2,)), dma,
            dma, dma((4,)), dma((4,)), dma, dma,
        ],
        compiler_params=pltpu.CompilerParams(
            has_side_effects=True, vmem_limit_bytes=60 * 1024 * 1024, collective_id=1
        ),
        cost_estimate=pl.CostEstimate(
            flops=10**10, bytes_accessed=10**7, transcendentals=10**7
        ),
    )(doc_lengths, queries, keys, values, out_weight, residual, norm_gain.reshape(1, D))


def body(
    queries, keys, values, doc_lengths, out_weight, residual, norm_gain, expert_ids,
    gate_values, w_gate, w_up, w_down,
):
    normed, hidden = front(queries, keys, values, doc_lengths, out_weight, residual, norm_gain)
    return routed_layer(normed, hidden, expert_ids, gate_values, w_gate, w_up, w_down)


def solution(mesh):
    in_specs = (
        P("seq", "exp"),
        P("seq", "exp"),
        P("seq", "exp"),
        P(),
        P("exp", "seq"),
        P(("seq", "exp"), None),
        P(),
        P(("seq", "exp"), None),
        P(("seq", "exp"), None),
        P(("seq", "exp"), None, None),
        P(("seq", "exp"), None, None),
        P(("seq", "exp"), None, None),
    )
    out_specs = P(("seq", "exp"), None)
    return jax.shard_map(body, mesh=mesh, in_specs=in_specs, out_specs=out_specs, check_vma=False)
```

```python
import functools

import jax
import jax.numpy as jnp
from jax import lax
from jax.experimental import pallas as pl
from jax.experimental.pallas import tpu as pltpu
from jax.sharding import PartitionSpec as P

HEAD_DIM = 128
SHARD = 512
BACK = 2048
NEG_FILL = -1e30
D = 4096
HALF = D // 2
FFH = 768
CAP = 9
TOPK = 8
DEVICES = 128
GROUPS = 4
PER_GROUP = DEVICES // GROUPS
MAIN = PER_GROUP * 8
ROWS = PER_GROUP * CAP
EXTRA = D // 16
MESSAGE = HALF + EXTRA
CHUNK = 512
STRIDE = 13
MESH = pl.DeviceIdType.MESH


def place():
    seq = lax.axis_index("seq")
    return seq // 8, (seq // 2) % 4, seq % 2, lax.axis_index("exp")


def device(y, x, c, z):
    return {"seq": (y * 4 + x) * 2 + c, "exp": z}


def line_axis(c, kind):
    even = jnp.where(kind == 3, 2, kind)
    odd = jnp.where(kind == 0, 2, jnp.where(kind == 3, 1, 0))
    return jnp.where(c == 0, even, odd)


def job_step(q):
    return jnp.where(q == 2, 3, jnp.where(q == 3, 2, q))


def along(axis, by):
    return jnp.where(axis == 1, by, 0), jnp.where(axis == 0, by, 0), jnp.where(axis == 2, by, 0)


def across(axis, d1, d2):
    ey = jnp.where(axis == 0, d1, jnp.where(axis == 1, 0, d2))
    ex = jnp.where(axis == 0, 0, jnp.where(axis == 1, d2, d1))
    ez = jnp.where(axis == 0, d2, jnp.where(axis == 1, d1, 0))
    return ey, ex, ez


def job_axis(q):
    y, x, c, z = place()
    return line_axis(c, (x + y + z + job_step(q)) % 4)


def job_block(q):
    y, x, c, z = place()
    ey, ex, ez = along(job_axis(q), job_step(q))
    return (y + ey) % 4, (x + ex) % 4, c, (z + ez) % 4


def job_target(q, n):
    y, x, c, z = place()
    m = (n * STRIDE) % PER_GROUP
    ey, ex, ez = across(job_axis(q), (m // 4) % 4, m % 4)
    return (y + ey) % 4, (x + ex) % 4, (c + m // 16) % 2, (z + ez) % 4


def job_source(q, n):
    y, x, c, z = place()
    m = (n * STRIDE) % PER_GROUP
    d1, d2 = (m // 4) % 4, m % 4
    sc = (c + m // 16) % 2
    kind = (x + y + z - d1 - d2 + 8) % 4
    ey, ex, ez = across(line_axis(sc, (kind + job_step(q)) % 4), d1, d2)
    return (y - ey + 4) % 4, (x - ex + 4) % 4, sc, (z - ez + 4) % 4


def job_target_ids(q):
    y, x, c, z = place()
    n = lax.broadcasted_iota(jnp.int32, (1, PER_GROUP), 1)
    m = (n * STRIDE) & (PER_GROUP - 1)
    ey, ex, ez = across(job_axis(q), (m >> 2) & 3, m & 3)
    ty, tx, tc, tz = (y + ey) & 3, (x + ex) & 3, (c + (m >> 4)) & 1, (z + ez) & 3
    return (((ty * 4 + tx) * 2 + tc) * 4 + tz).astype(jnp.float32)


def slot_of(row):
    return jnp.where(row < MAIN, row >> 3, row - MAIN), jnp.where(row < MAIN, row & 7, 8)


def moe_kernel(
    normed, hidden, ids_t, gates_t, w_gate, w_up, w_down, out,
    outbound, arrived, returned, wg, wu, wd, rows, extra, acc, perm, blocks, parts, meta, posn, gate,
    weight_sem, hidden_sem, send_sem, recv_sem, back_send_sem, back_recv_sem,
    line_send, line_recv, part_send, part_recv,
):
    tokens = normed.shape[0]
    y, x, c, z = place()
    meta[0] = jnp.transpose(
        jnp.concatenate(
            [
                ids_t[...].astype(jnp.float32), gates_t[...],
                jnp.zeros((tokens - 2 * TOPK, tokens), jnp.float32),
            ],
            axis=0,
        )
    )
    own_axis = line_axis(c, (x + y + z) % 4)
    for q, step in ((1, 1), (2, 3), (3, 2)):
        ey, ex, ez = along(own_axis, 4 - step)
        target = device((y + ey) % 4, (x + ex) % 4, c, (z + ez) % 4)
        for k, (src, dst) in enumerate(((meta.at[0], meta.at[q]), (normed, blocks.at[q - 1]))):
            pltpu.make_async_remote_copy(
                src_ref=src, dst_ref=dst, send_sem=line_send.at[k], recv_sem=line_recv.at[q - 1, k],
                device_id=target, device_id_type=MESH,
            ).start()
    loads = [
        pltpu.make_async_copy(src.at[0], dst, weight_sem.at[k])
        for k, (src, dst) in enumerate(((w_gate, wg), (w_up, wu), (w_down, wd)))
    ]
    for load in loads:
        load.start()
    line = lax.broadcasted_iota(jnp.int32, (16 * PER_GROUP, 16 * PER_GROUP), 0)
    other = lax.broadcasted_iota(jnp.int32, (16 * PER_GROUP, 16 * PER_GROUP), 1)
    perm[...] = (other == (line & (PER_GROUP - 1)) * 16 + (line >> 5)).astype(jnp.bfloat16)

    def pack(buffer, first, c, left, right):
        both = jnp.concatenate(
            [left.reshape(PER_GROUP, 8, CHUNK), right.reshape(PER_GROUP, 8, CHUNK)], axis=1
        )
        buffer[pl.ds(first, PER_GROUP), :, c : c + CHUNK] = both.astype(jnp.bfloat16)

    def pack_extra(buffer, first):
        stacked = jnp.concatenate(
            [extra[:, j * EXTRA : (j + 1) * EXTRA] for j in range(16)], axis=0
        ).astype(jnp.bfloat16)
        turned = lax.dot_general(
            perm[...], stacked, (((0,), (0,)), ((), ())), preferred_element_type=jnp.float32
        )
        buffer[pl.ds(first, PER_GROUP), :, HALF:MESSAGE] = turned.astype(jnp.bfloat16).reshape(
            PER_GROUP, 16, EXTRA
        )

    def unpack(buffer, first):
        for c in range(0, HALF, CHUNK):
            both = buffer[pl.ds(first, PER_GROUP), :, c : c + CHUNK].astype(jnp.float32)
            rows[0:MAIN, c : c + CHUNK] = both[:, 0:8].reshape(MAIN, CHUNK).astype(jnp.bfloat16)
            rows[0:MAIN, HALF + c : HALF + c + CHUNK] = (
                both[:, 8:16].reshape(MAIN, CHUNK).astype(jnp.bfloat16)
            )
        stacked = buffer[pl.ds(first, PER_GROUP), :, HALF:MESSAGE].reshape(PER_GROUP * 16, EXTRA)
        turned = jnp.dot(perm[...], stacked, preferred_element_type=jnp.float32)
        for j in range(16):
            rows[MAIN:ROWS, j * EXTRA : (j + 1) * EXTRA] = turned[
                j * PER_GROUP : (j + 1) * PER_GROUP
            ].astype(jnp.bfloat16)

    earlier = (
        lax.broadcasted_iota(jnp.int32, (tokens, tokens), 0)
        > lax.broadcasted_iota(jnp.int32, (tokens, tokens), 1)
    ).astype(jnp.bfloat16)

    def build(q, source):
        first = q * PER_GROUP
        target = job_target_ids(q)
        member = jnp.zeros((tokens, PER_GROUP), jnp.float32)
        weight = jnp.zeros((tokens, PER_GROUP), jnp.float32)
        for k in range(TOPK):
            hit = meta[q, :, k : k + 1] == target
            member = jnp.where(hit, 1.0, member)
            weight = jnp.where(hit, meta[q, :, TOPK + k : TOPK + k + 1], weight)
        count = jnp.dot(earlier, member.astype(jnp.bfloat16), preferred_element_type=jnp.float32)
        count = jnp.where(member > 0.0, count, -1.0)
        posn[q] = count
        gate[q] = weight
        row = lax.broadcasted_iota(jnp.int32, (ROWS, PER_GROUP), 0)
        message, _ = slot_of(row)
        spread = (message == lax.broadcasted_iota(jnp.int32, (ROWS, PER_GROUP), 1)).astype(
            jnp.bfloat16
        )
        picked = lax.dot_general(
            spread, count.astype(jnp.bfloat16), (((1,), (1,)), ((), ())),
            preferred_element_type=jnp.float32,
        )
        _, slot = slot_of(lax.broadcasted_iota(jnp.int32, (ROWS, tokens), 0))
        picks = (picked == slot.astype(jnp.float32)).astype(jnp.bfloat16)
        for c in range(0, HALF, CHUNK):
            halves = []
            for base in (c, HALF + c):
                got = jnp.dot(
                    picks, source[:, base : base + CHUNK], preferred_element_type=jnp.float32
                )
                extra[:, base : base + CHUNK] = got[MAIN:ROWS]
                halves.append(got[0:MAIN])
            pack(outbound, first, c, *halves)
        pack_extra(outbound, first)
        pltpu.make_async_copy(outbound.at[first], arrived.at[first], recv_sem.at[q]).start()

        def send(n, carry):
            pltpu.make_async_remote_copy(
                src_ref=outbound.at[first + n],
                dst_ref=arrived.at[first + n],
                send_sem=send_sem,
                recv_sem=recv_sem.at[q],
                device_id=device(*job_target(q, n)),
                device_id_type=MESH,
            ).start()
            return carry

        lax.fori_loop(1, PER_GROUP, send, 0)

    build(0, normed)

    def build_other(q, carry):
        for k, ref in enumerate((meta.at[0], normed)):
            pltpu.make_async_copy(ref, ref, line_recv.at[q - 1, k]).wait()
        build(q, blocks.at[q - 1])
        return carry

    lax.fori_loop(1, GROUPS, build_other, 0)
    for load in loads:
        load.wait()

    def expert(i, carry):
        q = (i + 1) % GROUPS
        first = q * PER_GROUP
        block = arrived.at[pl.ds(first, PER_GROUP)]
        pltpu.make_async_copy(block, block, recv_sem.at[q]).wait()
        unpack(arrived, first)
        gate_part = jnp.dot(rows[...], wg[...], preferred_element_type=jnp.float32)
        up_part = jnp.dot(rows[...], wu[...], preferred_element_type=jnp.float32)
        inner = (gate_part / (1.0 + jnp.exp(-gate_part)) * up_part).astype(jnp.bfloat16)
        for c in range(0, HALF, CHUNK):
            halves = []
            for base in (c, HALF + c):
                got = jnp.dot(
                    inner, wd[:, base : base + CHUNK], preferred_element_type=jnp.float32
                )
                extra[:, base : base + CHUNK] = got[MAIN:ROWS]
                halves.append(got[0:MAIN])
            pack(arrived, first, c, *halves)
        pack_extra(arrived, first)
        pltpu.make_async_copy(arrived.at[first], returned.at[first], back_recv_sem.at[q]).start()

        def send(n, carry):
            pltpu.make_async_remote_copy(
                src_ref=arrived.at[first + n],
                dst_ref=returned.at[first + n],
                send_sem=back_send_sem,
                recv_sem=back_recv_sem.at[q],
                device_id=device(*job_source(q, n)),
                device_id_type=MESH,
            ).start()
            return carry

        return lax.fori_loop(1, PER_GROUP, send, carry)

    lax.fori_loop(0, GROUPS, expert, 0)
    row = lax.broadcasted_iota(jnp.int32, (PER_GROUP, ROWS), 1)
    message, _ = slot_of(row)
    gather = (message == lax.broadcasted_iota(jnp.int32, (PER_GROUP, ROWS), 0)).astype(jnp.bfloat16)
    _, slot = slot_of(lax.broadcasted_iota(jnp.int32, (tokens, ROWS), 1))
    slot = slot.astype(jnp.float32)

    def combine(q):
        first = q * PER_GROUP
        block = returned.at[pl.ds(first, PER_GROUP)]
        pltpu.make_async_copy(block, block, back_recv_sem.at[q]).wait()
        unpack(returned, first)
        spread = functools.partial(jnp.dot, preferred_element_type=jnp.float32)
        used = spread(posn[q].astype(jnp.bfloat16), gather) == slot
        high = gate[q].astype(jnp.bfloat16)
        low = (gate[q] - high.astype(jnp.float32)).astype(jnp.bfloat16)
        both = jnp.concatenate(
            [jnp.where(used, spread(half, gather), 0.0) for half in (high, low)], axis=0
        ).astype(jnp.bfloat16)
        for c in range(0, D, CHUNK):
            got = jnp.dot(both, rows[:, c : c + CHUNK], preferred_element_type=jnp.float32)
            yield slice(c, c + CHUNK), got[0:tokens] + got[tokens : 2 * tokens]

    def combine_other(q, carry):
        for lanes, value in combine(q):
            blocks[q - 1, :, lanes] = value.astype(jnp.bfloat16)
        pltpu.make_async_remote_copy(
            src_ref=blocks.at[q - 1], dst_ref=parts.at[q - 1], send_sem=part_send,
            recv_sem=part_recv.at[q - 1], device_id=device(*job_block(q)), device_id_type=MESH,
        ).start()
        return carry

    lax.fori_loop(1, GROUPS, combine_other, 0)
    fetch = pltpu.make_async_copy(hidden, acc, hidden_sem)
    fetch.start()
    fetch.wait()
    for q in range(1, GROUPS):
        pltpu.make_async_copy(normed, normed, part_recv.at[q - 1]).wait()
        acc[...] += parts[q - 1].astype(jnp.float32)
    for lanes, value in combine(0):
        out[:, lanes] = (acc[:, lanes] + value).astype(jnp.bfloat16)
    for k, ref in enumerate((meta.at[pl.ds(0, 3)], blocks)):
        pltpu.make_async_copy(ref, ref, line_send.at[k]).wait()
    pltpu.make_async_copy(blocks, blocks, part_send).wait()
    sent = outbound.at[pl.ds(0, DEVICES - GROUPS)]
    for sem in (send_sem, back_send_sem):
        pltpu.make_async_copy(sent, sent, sem).wait()


def routed_layer(normed, hidden, expert_ids, gate_values, w_gate, w_up, w_down):
    tokens = normed.shape[0]
    vmem = pl.BlockSpec(memory_space=pltpu.VMEM)
    anywhere = pl.BlockSpec(memory_space=pl.ANY)
    dma = pltpu.SemaphoreType.DMA
    messages = pltpu.VMEM((DEVICES, 16, MESSAGE), jnp.bfloat16)
    return pl.pallas_call(
        moe_kernel,
        out_shape=jax.ShapeDtypeStruct((tokens, D), jnp.bfloat16),
        in_specs=[vmem, anywhere, vmem, vmem] + [anywhere] * 3,
        out_specs=vmem,
        scratch_shapes=[
            messages, messages, messages,
            pltpu.VMEM((D, FFH), jnp.bfloat16),
            pltpu.VMEM((D, FFH), jnp.bfloat16),
            pltpu.VMEM((FFH, D), jnp.bfloat16),
            pltpu.VMEM((ROWS, D), jnp.bfloat16),
            pltpu.VMEM((PER_GROUP, D), jnp.float32),
            pltpu.VMEM((tokens, D), jnp.float32),
            pltpu.VMEM((16 * PER_GROUP, 16 * PER_GROUP), jnp.bfloat16),
            pltpu.VMEM((GROUPS - 1, tokens, D), jnp.bfloat16),
            pltpu.VMEM((GROUPS - 1, tokens, D), jnp.bfloat16),
            pltpu.VMEM((GROUPS, tokens, 128), jnp.float32),
            pltpu.VMEM((GROUPS, tokens, PER_GROUP), jnp.float32),
            pltpu.VMEM((GROUPS, tokens, PER_GROUP), jnp.float32),
            dma((3,)), dma, dma, dma((GROUPS,)), dma, dma((GROUPS,)),
            dma((2,)), dma((GROUPS - 1, 2)), dma, dma((GROUPS - 1,)),
        ],
        compiler_params=pltpu.CompilerParams(
            has_side_effects=True, vmem_limit_bytes=64 * 1024 * 1024
        ),
        cost_estimate=pl.CostEstimate(
            flops=24 * 10**9, bytes_accessed=40 * 10**6, transcendentals=10**6
        ),
    )(normed, hidden, expert_ids.T, gate_values.T, w_gate, w_up, w_down)


def rotated(chip, by):
    return (chip + by) % 16


def chip_device(chip, c, z):
    return device(chip // 4, chip % 4, c, z)


def remote(src, dst, send_sem, recv_sem, target):
    return pltpu.make_async_remote_copy(
        src_ref=src, dst_ref=dst, send_sem=send_sem, recv_sem=recv_sem,
        device_id=target, device_id_type=MESH,
    )


def wait_bytes(ref, sem):
    pltpu.make_async_copy(ref, ref, sem).wait()


def front_kernel(
    doc_lengths, queries, keys, values, out_weight, residual, gain, normed, hidden,
    kv, weight, att, relay, stage, fin, tops, totals, sums,
    kv_send, kv_recv, line_recv, line_fwd, plane_recv, plane_fwd, weight_send,
    att_send, att_recv, relay_recv, fin_recv, term_send,
):
    y, x, c, z = place()
    chip = y * 4 + x
    partner = device(y, x, 1 - c, z)
    barrier = pltpu.get_barrier_semaphore()
    peers = [partner]
    for by in (1, 2, 14, 15):
        peers.append(chip_device(rotated(chip, by), c, z))
    for by in (1, 3):
        peers.append(device(y, (x + by) % 4, c, z))
        peers.append(device((y + by) % 4, x, c, z))
        peers.append(device(y, x, c, (z + by) % 4))
        peers.append(device(y, x, 1 - c, (z + by) % 4))
    for peer in peers:
        pl.semaphore_signal(barrier, inc=1, device_id=peer, device_id_type=MESH)
    pl.semaphore_wait(barrier, len(peers))

    def kv_slot(slot):
        return kv.at[pl.ds(pl.multiple_of(slot * SHARD, SHARD), SHARD)]

    weight[chip] = out_weight[...]

    def spread(u):
        block = weight.at[4 * y + u]
        for way, step in enumerate((1, 3)):
            remote(
                block, block, weight_send, plane_recv.at[way], device((y + step) % 4, x, c, z)
            ).start()

    for way, step in enumerate((1, 3)):
        block = weight.at[chip]
        remote(
            block, block, weight_send, line_recv.at[way], device(y, (x + step) % 4, c, z)
        ).start()
    spread(x)
    own = pl.ds(pl.multiple_of((4 + c) * SHARD, SHARD), SHARD)
    kv[own, 0:HEAD_DIM] = keys[...]
    kv[own, HEAD_DIM : 2 * HEAD_DIM] = values[...]
    for ahead in (1, 2):
        remote(
            kv_slot(4 + c), kv_slot(4 - 2 * ahead + c), kv_send, kv_recv.at[ahead - 1],
            chip_device(rotated(chip, ahead), c, z),
        ).start()

    def line_step():
        for way, step in enumerate((1, 3)):
            wait_bytes(weight.at[0], line_recv.at[way])
            came = (x - step + 4) % 4
            part = weight.at[4 * y + came, pl.ds(512 * way, 512)]
            remote(
                part, part, weight_send, line_fwd.at[way], device(y, (x + step) % 4, c, z)
            ).start()
            spread(came)

    def line_end():
        for way in (0, 1):
            wait_bytes(weight.at[0, pl.ds(0, 512)], line_fwd.at[way])
        spread((x + 2) % 4)

    def plane_step(way):
        step = (1, 3)[way]
        wait_bytes(weight.at[pl.ds(0, 4)], plane_recv.at[way])
        came = (y - step + 4) % 4
        part = weight.at[pl.ds(4 * came, 4), pl.ds(512 * way, 512)]
        remote(
            part, part, weight_send, plane_fwd.at[way], device((y + step) % 4, x, c, z)
        ).start()

    def plane_end():
        for way in (0, 1):
            wait_bytes(weight.at[pl.ds(0, 4), pl.ds(0, 512)], plane_fwd.at[way])

    def hand_over(slot, sem):
        remote(kv_slot(slot), kv_slot(slot), kv_send, kv_recv.at[sem], partner).start()

    pl.when(c == 0)(lambda: hand_over(4, 2))
    ends = []
    total_len = doc_lengths[0]
    for i in range(doc_lengths.shape[0]):
        if i:
            total_len = total_len + doc_lengths[i]
        ends.append(total_len)
    factor = HEAD_DIM ** (-0.5) * 1.4426950408889634

    def row_of(j):
        return (y + (0, 3, 1, 2)[j]) % 4

    def term(i, j):
        columns = [weight[4 * row_of(j) + u] for u in range(4)]
        return jnp.dot(
            att[i].reshape(256, 1024), jnp.concatenate(columns, axis=1),
            preferred_element_type=jnp.float32,
        )

    def put(i, j, value):
        at = (i * 4 + row_of(j)) * 2
        stage[pl.ds(at, 2)] = value.astype(jnp.bfloat16).reshape(2, 128, 512)
        return at

    up, down = (z + 1) % 4, (z + 3) % 4

    def deliver(i, j, value):
        at = put(i, j, value)
        for tc in (0, 1):
            remote(
                stage.at[at + tc], fin.at[((i - 1) * 2 + c) * 4 + row_of(j)], term_send, fin_recv,
                device(y, x, tc, (up, down)[i - 1]),
            ).start()

    def relay_out(j):
        at = put(0, j, term(0, j))
        remote(
            stage.at[pl.ds(at, 2)], relay.at[pl.ds(2 * row_of(j), 2)], term_send, relay_recv.at[j],
            device(y, x, c, (up, down)[j % 2]),
        ).start()

    def direct(i, j):
        deliver(i, j, term(i, j))

    def relayed(i, j):
        value = term(i, j)
        wait_bytes(relay.at[pl.ds(0, 2)], relay_recv.at[j])
        passed = relay[pl.ds(2 * row_of(j), 2)].reshape(256, 512)
        deliver(i, j, value + passed.astype(jnp.float32))

    def keep(j):
        at = put(3, j, term(3, j))
        spot = (4 + c) * 4 + row_of(j)
        fin[spot] = stage[at + c]
        remote(stage.at[at + 1 - c], fin.at[spot], term_send, fin_recv, partner).start()

    def after_far():
        wait_bytes(stage.at[pl.ds(0, 2)], att_recv.at[0])
        relay_out(0)
        plane_step(0)
        plane_step(1)
        relay_out(1)
        relay_out(2)

    def after_up():
        wait_bytes(stage.at[pl.ds(0, 2)], att_recv.at[1])
        relayed(1, 0)
        direct(1, 1)

    def after_down():
        wait_bytes(stage.at[pl.ds(0, 2)], att_recv.at[2])
        direct(2, 0)
        direct(2, 2)
        relayed(2, 1)
        relayed(1, 2)

    def after_own():
        wait_bytes(stage.at[pl.ds(0, 2)], att_recv.at[3])
        plane_end()
        relay_out(3)
        direct(1, 3)
        for j in range(4):
            keep(j)
        relayed(2, 3)

    def attend(slots, first, last):
        held = [kv_slot(slot) for slot in slots]
        starts = [(chip - 2) * 2 * SHARD + slot * SHARD for slot in slots]

        def block(i, carry):
            b = (z + jnp.where(i == 2, 3, jnp.where(i == 3, 0, 2 - i))) % 4
            pos = (chip * 2 + c) * SHARD + b * 128 + lax.broadcasted_iota(jnp.int32, (128, 1), 0)
            low = jnp.zeros((128, 1), jnp.int32)
            for end in ends:
                low = jnp.where(pos >= end, end, low)
            low = jnp.concatenate([low, low], axis=0)
            high = jnp.concatenate([pos, pos], axis=0)

            def heads(hp):
                n = i * 4 + hp
                lanes = hp * 256
                both = queries[pl.ds(pl.multiple_of(b * 128, 128), 128), pl.ds(lanes, 256)]
                q = jnp.concatenate([both[:, 0:128], both[:, 128:256]], axis=0)
                at = lax.broadcasted_iota(jnp.int32, (256, SHARD), 1)
                scores, top = [], None
                for ref, start in zip(held, starts):
                    part = lax.dot_general(
                        q, ref[:, 0:HEAD_DIM], (((1,), (1,)), ((), ())),
                        preferred_element_type=jnp.float32,
                    )
                    seen = at >= low - start
                    if first:
                        seen = seen & (at <= high - start)
                    part = jnp.where(seen, part, NEG_FILL)
                    peak = jnp.max(part, axis=1, keepdims=True)
                    top = peak if top is None else jnp.maximum(top, peak)
                    scores.append(part)
                if not first:
                    old = tops[n][:, 0:1]
                    top = jnp.maximum(top, old)
                    shrink = jnp.exp2((old - top) * factor)
                    total = totals[n][:, 0:1] * shrink
                    got = sums[n] * shrink
                for part, ref in zip(scores, held):
                    weights = jnp.exp2((part - top) * factor)
                    more = jnp.sum(weights, axis=1, keepdims=True)
                    value = jnp.dot(
                        weights.astype(jnp.bfloat16), ref[:, HEAD_DIM : 2 * HEAD_DIM],
                        preferred_element_type=jnp.float32,
                    )
                    if first:
                        total, got = more, value
                    else:
                        total, got = total + more, got + value
                if not last:
                    tops[n] = jnp.broadcast_to(top, (256, 128))
                    totals[n] = jnp.broadcast_to(total, (256, 128))
                    sums[n] = got
                else:
                    got = (got / total).astype(jnp.bfloat16)
                    att[i, c, :, pl.ds(lanes, 256)] = jnp.concatenate(
                        [got[0:128], got[128:256]], axis=1
                    )

            for hp in range(4):
                heads(hp)
                if last and hp == 1:
                    for k, then in enumerate((after_far, after_up, after_down)):
                        pl.when(i == k + 1)(then)
            if last:
                remote(att.at[i, c], att.at[i, c], att_send, att_recv.at[i], partner).start()
            return carry

        lax.fori_loop(0, 4, block, 0)

    attend([4 + c], True, False)
    line_step()
    wait_bytes(kv_slot(0), kv_recv.at[0])
    hand_over(2 + c, 3)
    wait_bytes(kv_slot(0), kv_recv.at[3])
    attend([2, 3], False, False)
    line_end()
    wait_bytes(kv_slot(0), kv_recv.at[1])
    pl.when(c == 1)(lambda: hand_over(1, 2))
    wait_bytes(kv_slot(0), kv_recv.at[2])
    attend([jnp.where(c == 0, 0, 4), 1], False, True)
    after_own()
    wait_bytes(fin.at[pl.ds(0, 20)], fin_recv)
    squares = jnp.zeros((128, HEAD_DIM), jnp.float32)
    for cs in (0, 1):
        for k in range(16):
            r, u = k // 4, k % 4
            lanes = slice((2 * k + cs) * 128, (2 * k + cs + 1) * 128)
            value = residual[:, lanes].astype(jnp.float32)
            for side in range(3):
                value = value + fin[
                    (side * 2 + cs) * 4 + r, :, u * 128 : (u + 1) * 128
                ].astype(jnp.float32)
            hidden[:, lanes] = value
            squares = squares + value * value
    variance = jnp.sum(squares, axis=1, keepdims=True) * (1.0 / D)
    shrink = lax.rsqrt(variance + 1e-06)
    for first in range(0, D, CHUNK):
        lanes = slice(first, first + CHUNK)
        normed[:, lanes] = (hidden[:, lanes] * shrink * gain[:, lanes]).astype(jnp.bfloat16)

    for _ in range(4):
        wait_bytes(kv_slot(0), kv_send)
    wait_bytes(weight.at[pl.ds(0, 15)], weight_send)
    wait_bytes(stage.at[pl.ds(0, 8)], att_send)
    wait_bytes(stage.at[pl.ds(0, 28)], term_send)


def front(queries, keys, values, doc_lengths, out_weight, residual, norm_gain):
    vmem = pl.BlockSpec(memory_space=pltpu.VMEM)
    dma = pltpu.SemaphoreType.DMA
    tokens = residual.shape[0]
    return pl.pallas_call(
        front_kernel,
        out_shape=(
            jax.ShapeDtypeStruct((tokens, D), jnp.bfloat16),
            jax.ShapeDtypeStruct((tokens, D), jnp.float32),
        ),
        in_specs=[pl.BlockSpec(memory_space=pltpu.SMEM)] + [vmem] * 6,
        out_specs=(vmem, vmem),
        scratch_shapes=[
            pltpu.VMEM((6 * SHARD, 2 * HEAD_DIM), jnp.bfloat16),
            pltpu.VMEM((16, 1024, HEAD_DIM), jnp.bfloat16),
            pltpu.VMEM((4, 2, 128, 1024), jnp.bfloat16),
            pltpu.VMEM((8, 128, 512), jnp.bfloat16),
            pltpu.VMEM((32, 128, 512), jnp.bfloat16),
            pltpu.VMEM((24, 128, 512), jnp.bfloat16),
            pltpu.VMEM((16, 256, 128), jnp.float32),
            pltpu.VMEM((16, 256, 128), jnp.float32),
            pltpu.VMEM((16, 256, 128), jnp.float32),
            dma, dma((4,)), dma((2,)), dma((2,)), dma((2,)), dma((2,)), dma,
            dma, dma((4,)), dma((4,)), dma, dma,
        ],
        compiler_params=pltpu.CompilerParams(
            has_side_effects=True, vmem_limit_bytes=60 * 1024 * 1024, collective_id=1
        ),
        cost_estimate=pl.CostEstimate(
            flops=10**10, bytes_accessed=10**7, transcendentals=10**7
        ),
    )(doc_lengths, queries, keys, values, out_weight, residual, norm_gain.reshape(1, D))


def body(
    queries, keys, values, doc_lengths, out_weight, residual, norm_gain, expert_ids,
    gate_values, w_gate, w_up, w_down,
):
    normed, hidden = front(queries, keys, values, doc_lengths, out_weight, residual, norm_gain)
    return routed_layer(normed, hidden, expert_ids, gate_values, w_gate, w_up, w_down)


def solution(mesh):
    in_specs = (
        P("seq", "exp"),
        P("seq", "exp"),
        P("seq", "exp"),
        P(),
        P("exp", "seq"),
        P(("seq", "exp"), None),
        P(),
        P(("seq", "exp"), None),
        P(("seq", "exp"), None),
        P(("seq", "exp"), None, None),
        P(("seq", "exp"), None, None),
        P(("seq", "exp"), None, None),
    )
    out_specs = P(("seq", "exp"), None)
    return jax.shard_map(body, mesh=mesh, in_specs=in_specs, out_specs=out_specs, check_vma=False)
```

```python
import functools

import jax
import jax.numpy as jnp
from jax import lax
from jax.experimental import pallas as pl
from jax.experimental.pallas import tpu as pltpu
from jax.sharding import PartitionSpec as P

HEAD_DIM = 128
SHARD = 512
BACK = 2048
NEG_FILL = -1e30
D = 4096
HALF = D // 2
FFH = 768
CAP = 9
TOPK = 8
DEVICES = 128
GROUPS = 4
PER_GROUP = DEVICES // GROUPS
MAIN = PER_GROUP * 8
ROWS = PER_GROUP * CAP
EXTRA = D // 16
MESSAGE = HALF + EXTRA
CHUNK = 512
STRIDE = 13
MESH = pl.DeviceIdType.MESH


def place():
    seq = lax.axis_index("seq")
    return seq // 8, (seq // 2) % 4, seq % 2, lax.axis_index("exp")


def device(y, x, c, z):
    return {"seq": (y * 4 + x) * 2 + c, "exp": z}


def line_axis(c, kind):
    even = jnp.where(kind == 3, 2, kind)
    odd = jnp.where(kind == 0, 2, jnp.where(kind == 3, 1, 0))
    return jnp.where(c == 0, even, odd)


def job_step(q):
    return jnp.where(q == 2, 3, jnp.where(q == 3, 2, q))


def along(axis, by):
    return jnp.where(axis == 1, by, 0), jnp.where(axis == 0, by, 0), jnp.where(axis == 2, by, 0)


def across(axis, d1, d2):
    ey = jnp.where(axis == 0, d1, jnp.where(axis == 1, 0, d2))
    ex = jnp.where(axis == 0, 0, jnp.where(axis == 1, d2, d1))
    ez = jnp.where(axis == 0, d2, jnp.where(axis == 1, d1, 0))
    return ey, ex, ez


def job_axis(q):
    y, x, c, z = place()
    return line_axis(c, (x + y + z + job_step(q)) % 4)


def job_block(q):
    y, x, c, z = place()
    ey, ex, ez = along(job_axis(q), job_step(q))
    return (y + ey) % 4, (x + ex) % 4, c, (z + ez) % 4


def job_target(q, n):
    y, x, c, z = place()
    m = (n * STRIDE) % PER_GROUP
    ey, ex, ez = across(job_axis(q), (m // 4) % 4, m % 4)
    return (y + ey) % 4, (x + ex) % 4, (c + m // 16) % 2, (z + ez) % 4


def job_source(q, n):
    y, x, c, z = place()
    m = (n * STRIDE) % PER_GROUP
    d1, d2 = (m // 4) % 4, m % 4
    sc = (c + m // 16) % 2
    kind = (x + y + z - d1 - d2 + 8) % 4
    ey, ex, ez = across(line_axis(sc, (kind + job_step(q)) % 4), d1, d2)
    return (y - ey + 4) % 4, (x - ex + 4) % 4, sc, (z - ez + 4) % 4


def job_target_ids(q):
    y, x, c, z = place()
    n = lax.broadcasted_iota(jnp.int32, (1, PER_GROUP), 1)
    m = (n * STRIDE) & (PER_GROUP - 1)
    ey, ex, ez = across(job_axis(q), (m >> 2) & 3, m & 3)
    ty, tx, tc, tz = (y + ey) & 3, (x + ex) & 3, (c + (m >> 4)) & 1, (z + ez) & 3
    return (((ty * 4 + tx) * 2 + tc) * 4 + tz).astype(jnp.float32)


def slot_of(row):
    return jnp.where(row < MAIN, row >> 3, row - MAIN), jnp.where(row < MAIN, row & 7, 8)


def moe_kernel(
    normed, hidden, ids_t, gates_t, w_gate, w_up, w_down, out,
    outbound, arrived, returned, wg, wu, wd, rows, extra, acc, perm, blocks, parts, meta, posn, gate,
    weight_sem, hidden_sem, send_sem, recv_sem, back_send_sem, back_recv_sem,
    line_send, line_recv, part_send, part_recv,
):
    tokens = normed.shape[0]
    y, x, c, z = place()
    meta[0] = jnp.transpose(
        jnp.concatenate(
            [
                ids_t[...].astype(jnp.float32), gates_t[...],
                jnp.zeros((tokens - 2 * TOPK, tokens), jnp.float32),
            ],
            axis=0,
        )
    )
    own_axis = line_axis(c, (x + y + z) % 4)
    for q, step in ((1, 1), (2, 3), (3, 2)):
        ey, ex, ez = along(own_axis, 4 - step)
        target = device((y + ey) % 4, (x + ex) % 4, c, (z + ez) % 4)
        for k, (src, dst) in enumerate(((meta.at[0], meta.at[q]), (normed, blocks.at[q - 1]))):
            pltpu.make_async_remote_copy(
                src_ref=src, dst_ref=dst, send_sem=line_send.at[k], recv_sem=line_recv.at[q - 1, k],
                device_id=target, device_id_type=MESH,
            ).start()
    loads = [
        pltpu.make_async_copy(src.at[0], dst, weight_sem.at[k])
        for k, (src, dst) in enumerate(((w_gate, wg), (w_up, wu), (w_down, wd)))
    ]
    for load in loads:
        load.start()
    line = lax.broadcasted_iota(jnp.int32, (16 * PER_GROUP, 16 * PER_GROUP), 0)
    other = lax.broadcasted_iota(jnp.int32, (16 * PER_GROUP, 16 * PER_GROUP), 1)
    perm[...] = (other == (line & (PER_GROUP - 1)) * 16 + (line >> 5)).astype(jnp.bfloat16)

    def pack(buffer, first, c, left, right):
        both = jnp.concatenate(
            [left.reshape(PER_GROUP, 8, CHUNK), right.reshape(PER_GROUP, 8, CHUNK)], axis=1
        )
        buffer[pl.ds(first, PER_GROUP), :, c : c + CHUNK] = both.astype(jnp.bfloat16)

    def pack_extra(buffer, first):
        stacked = jnp.concatenate(
            [extra[:, j * EXTRA : (j + 1) * EXTRA] for j in range(16)], axis=0
        ).astype(jnp.bfloat16)
        turned = lax.dot_general(
            perm[...], stacked, (((0,), (0,)), ((), ())), preferred_element_type=jnp.float32
        )
        buffer[pl.ds(first, PER_GROUP), :, HALF:MESSAGE] = turned.astype(jnp.bfloat16).reshape(
            PER_GROUP, 16, EXTRA
        )

    def unpack(buffer, first):
        for c in range(0, HALF, CHUNK):
            both = buffer[pl.ds(first, PER_GROUP), :, c : c + CHUNK].astype(jnp.float32)
            rows[0:MAIN, c : c + CHUNK] = both[:, 0:8].reshape(MAIN, CHUNK).astype(jnp.bfloat16)
            rows[0:MAIN, HALF + c : HALF + c + CHUNK] = (
                both[:, 8:16].reshape(MAIN, CHUNK).astype(jnp.bfloat16)
            )
        stacked = buffer[pl.ds(first, PER_GROUP), :, HALF:MESSAGE].reshape(PER_GROUP * 16, EXTRA)
        turned = jnp.dot(perm[...], stacked, preferred_element_type=jnp.float32)
        for j in range(16):
            rows[MAIN:ROWS, j * EXTRA : (j + 1) * EXTRA] = turned[
                j * PER_GROUP : (j + 1) * PER_GROUP
            ].astype(jnp.bfloat16)

    earlier = (
        lax.broadcasted_iota(jnp.int32, (tokens, tokens), 0)
        > lax.broadcasted_iota(jnp.int32, (tokens, tokens), 1)
    ).astype(jnp.bfloat16)

    def build(q, source):
        first = q * PER_GROUP
        target = job_target_ids(q)
        member = jnp.zeros((tokens, PER_GROUP), jnp.float32)
        weight = jnp.zeros((tokens, PER_GROUP), jnp.float32)
        for k in range(TOPK):
            hit = meta[q, :, k : k + 1] == target
            member = jnp.where(hit, 1.0, member)
            weight = jnp.where(hit, meta[q, :, TOPK + k : TOPK + k + 1], weight)
        count = jnp.dot(earlier, member.astype(jnp.bfloat16), preferred_element_type=jnp.float32)
        count = jnp.where(member > 0.0, count, -1.0)
        posn[q] = count
        gate[q] = weight
        row = lax.broadcasted_iota(jnp.int32, (ROWS, PER_GROUP), 0)
        message, _ = slot_of(row)
        spread = (message == lax.broadcasted_iota(jnp.int32, (ROWS, PER_GROUP), 1)).astype(
            jnp.bfloat16
        )
        picked = lax.dot_general(
            spread, count.astype(jnp.bfloat16), (((1,), (1,)), ((), ())),
            preferred_element_type=jnp.float32,
        )
        _, slot = slot_of(lax.broadcasted_iota(jnp.int32, (ROWS, tokens), 0))
        picks = (picked == slot.astype(jnp.float32)).astype(jnp.bfloat16)
        for c in range(0, HALF, CHUNK):
            halves = []
            for base in (c, HALF + c):
                got = jnp.dot(
                    picks, source[:, base : base + CHUNK], preferred_element_type=jnp.float32
                )
                extra[:, base : base + CHUNK] = got[MAIN:ROWS]
                halves.append(got[0:MAIN])
            pack(outbound, first, c, *halves)
        pack_extra(outbound, first)
        pltpu.make_async_copy(outbound.at[first], arrived.at[first], recv_sem.at[q]).start()

        def send(n, carry):
            pltpu.make_async_remote_copy(
                src_ref=outbound.at[first + n],
                dst_ref=arrived.at[first + n],
                send_sem=send_sem,
                recv_sem=recv_sem.at[q],
                device_id=device(*job_target(q, n)),
                device_id_type=MESH,
            ).start()
            return carry

        lax.fori_loop(1, PER_GROUP, send, 0)

    build(0, normed)

    def build_other(q, carry):
        for k, ref in enumerate((meta.at[0], normed)):
            pltpu.make_async_copy(ref, ref, line_recv.at[q - 1, k]).wait()
        build(q, blocks.at[q - 1])
        return carry

    lax.fori_loop(1, GROUPS, build_other, 0)
    for load in loads:
        load.wait()

    def expert(i, carry):
        q = (i + 1) % GROUPS
        first = q * PER_GROUP
        block = arrived.at[pl.ds(first, PER_GROUP)]
        pltpu.make_async_copy(block, block, recv_sem.at[q]).wait()
        unpack(arrived, first)
        gate_part = jnp.dot(rows[...], wg[...], preferred_element_type=jnp.float32)
        up_part = jnp.dot(rows[...], wu[...], preferred_element_type=jnp.float32)
        inner = (gate_part / (1.0 + jnp.exp(-gate_part)) * up_part).astype(jnp.bfloat16)
        for c in range(0, HALF, CHUNK):
            halves = []
            for base in (c, HALF + c):
                got = jnp.dot(
                    inner, wd[:, base : base + CHUNK], preferred_element_type=jnp.float32
                )
                extra[:, base : base + CHUNK] = got[MAIN:ROWS]
                halves.append(got[0:MAIN])
            pack(arrived, first, c, *halves)
        pack_extra(arrived, first)
        pltpu.make_async_copy(arrived.at[first], returned.at[first], back_recv_sem.at[q]).start()

        def send(n, carry):
            pltpu.make_async_remote_copy(
                src_ref=arrived.at[first + n],
                dst_ref=returned.at[first + n],
                send_sem=back_send_sem,
                recv_sem=back_recv_sem.at[q],
                device_id=device(*job_source(q, n)),
                device_id_type=MESH,
            ).start()
            return carry

        return lax.fori_loop(1, PER_GROUP, send, carry)

    lax.fori_loop(0, GROUPS, expert, 0)
    row = lax.broadcasted_iota(jnp.int32, (PER_GROUP, ROWS), 1)
    message, _ = slot_of(row)
    gather = (message == lax.broadcasted_iota(jnp.int32, (PER_GROUP, ROWS), 0)).astype(jnp.bfloat16)
    _, slot = slot_of(lax.broadcasted_iota(jnp.int32, (tokens, ROWS), 1))
    slot = slot.astype(jnp.float32)

    def combine(q):
        first = q * PER_GROUP
        block = returned.at[pl.ds(first, PER_GROUP)]
        pltpu.make_async_copy(block, block, back_recv_sem.at[q]).wait()
        unpack(returned, first)
        spread = functools.partial(jnp.dot, preferred_element_type=jnp.float32)
        used = spread(posn[q].astype(jnp.bfloat16), gather) == slot
        high = gate[q].astype(jnp.bfloat16)
        low = (gate[q] - high.astype(jnp.float32)).astype(jnp.bfloat16)
        both = jnp.concatenate(
            [jnp.where(used, spread(half, gather), 0.0) for half in (high, low)], axis=0
        ).astype(jnp.bfloat16)
        for c in range(0, D, CHUNK):
            got = jnp.dot(both, rows[:, c : c + CHUNK], preferred_element_type=jnp.float32)
            yield slice(c, c + CHUNK), got[0:tokens] + got[tokens : 2 * tokens]

    def combine_other(q, carry):
        for lanes, value in combine(q):
            blocks[q - 1, :, lanes] = value.astype(jnp.bfloat16)
        pltpu.make_async_remote_copy(
            src_ref=blocks.at[q - 1], dst_ref=parts.at[q - 1], send_sem=part_send,
            recv_sem=part_recv.at[q - 1], device_id=device(*job_block(q)), device_id_type=MESH,
        ).start()
        return carry

    lax.fori_loop(1, GROUPS, combine_other, 0)
    fetch = pltpu.make_async_copy(hidden, acc, hidden_sem)
    fetch.start()
    fetch.wait()
    for lanes, value in combine(0):
        acc[:, lanes] += value
    for q in range(1, GROUPS):
        pltpu.make_async_copy(normed, normed, part_recv.at[q - 1]).wait()
    for c in range(0, D, CHUNK):
        lanes = slice(c, c + CHUNK)
        value = acc[:, lanes]
        for q in range(1, GROUPS):
            value = value + parts[q - 1, :, lanes].astype(jnp.float32)
        out[:, lanes] = value.astype(jnp.bfloat16)
    for k, ref in enumerate((meta.at[pl.ds(0, 3)], blocks)):
        pltpu.make_async_copy(ref, ref, line_send.at[k]).wait()
    pltpu.make_async_copy(blocks, blocks, part_send).wait()
    sent = outbound.at[pl.ds(0, DEVICES - GROUPS)]
    for sem in (send_sem, back_send_sem):
        pltpu.make_async_copy(sent, sent, sem).wait()


def routed_layer(normed, hidden, expert_ids, gate_values, w_gate, w_up, w_down):
    tokens = normed.shape[0]
    vmem = pl.BlockSpec(memory_space=pltpu.VMEM)
    anywhere = pl.BlockSpec(memory_space=pl.ANY)
    dma = pltpu.SemaphoreType.DMA
    messages = pltpu.VMEM((DEVICES, 16, MESSAGE), jnp.bfloat16)
    return pl.pallas_call(
        moe_kernel,
        out_shape=jax.ShapeDtypeStruct((tokens, D), jnp.bfloat16),
        in_specs=[vmem, anywhere, vmem, vmem] + [anywhere] * 3,
        out_specs=vmem,
        scratch_shapes=[
            messages, messages, messages,
            pltpu.VMEM((D, FFH), jnp.bfloat16),
            pltpu.VMEM((D, FFH), jnp.bfloat16),
            pltpu.VMEM((FFH, D), jnp.bfloat16),
            pltpu.VMEM((ROWS, D), jnp.bfloat16),
            pltpu.VMEM((PER_GROUP, D), jnp.float32),
            pltpu.VMEM((tokens, D), jnp.float32),
            pltpu.VMEM((16 * PER_GROUP, 16 * PER_GROUP), jnp.bfloat16),
            pltpu.VMEM((GROUPS - 1, tokens, D), jnp.bfloat16),
            pltpu.VMEM((GROUPS - 1, tokens, D), jnp.bfloat16),
            pltpu.VMEM((GROUPS, tokens, 128), jnp.float32),
            pltpu.VMEM((GROUPS, tokens, PER_GROUP), jnp.float32),
            pltpu.VMEM((GROUPS, tokens, PER_GROUP), jnp.float32),
            dma((3,)), dma, dma, dma((GROUPS,)), dma, dma((GROUPS,)),
            dma((2,)), dma((GROUPS - 1, 2)), dma, dma((GROUPS - 1,)),
        ],
        compiler_params=pltpu.CompilerParams(
            has_side_effects=True, vmem_limit_bytes=64 * 1024 * 1024
        ),
        cost_estimate=pl.CostEstimate(
            flops=24 * 10**9, bytes_accessed=40 * 10**6, transcendentals=10**6
        ),
    )(normed, hidden, expert_ids.T, gate_values.T, w_gate, w_up, w_down)


def rotated(chip, by):
    return (chip + by) % 16


def chip_device(chip, c, z):
    return device(chip // 4, chip % 4, c, z)


def remote(src, dst, send_sem, recv_sem, target):
    return pltpu.make_async_remote_copy(
        src_ref=src, dst_ref=dst, send_sem=send_sem, recv_sem=recv_sem,
        device_id=target, device_id_type=MESH,
    )


def wait_bytes(ref, sem):
    pltpu.make_async_copy(ref, ref, sem).wait()


def front_kernel(
    doc_lengths, queries, keys, values, out_weight, residual, gain, normed, hidden,
    kv, weight, att, relay, stage, fin, tops, totals, sums,
    kv_send, kv_recv, line_recv, line_fwd, plane_recv, plane_fwd, weight_send,
    att_send, att_recv, relay_recv, fin_recv, term_send,
):
    y, x, c, z = place()
    chip = y * 4 + x
    partner = device(y, x, 1 - c, z)
    barrier = pltpu.get_barrier_semaphore()
    peers = [partner]
    for by in (1, 2, 14, 15):
        peers.append(chip_device(rotated(chip, by), c, z))
    for by in (1, 3):
        peers.append(device(y, (x + by) % 4, c, z))
        peers.append(device((y + by) % 4, x, c, z))
        peers.append(device(y, x, c, (z + by) % 4))
        peers.append(device(y, x, 1 - c, (z + by) % 4))
    for peer in peers:
        pl.semaphore_signal(barrier, inc=1, device_id=peer, device_id_type=MESH)
    pl.semaphore_wait(barrier, len(peers))

    def kv_slot(slot):
        return kv.at[pl.ds(pl.multiple_of(slot * SHARD, SHARD), SHARD)]

    own = pl.ds(pl.multiple_of((4 + c) * SHARD, SHARD), SHARD)
    kv[own, 0:HEAD_DIM] = keys[...]
    kv[own, HEAD_DIM : 2 * HEAD_DIM] = values[...]

    def send_kv(ahead):
        remote(
            kv_slot(4 + c), kv_slot(4 - 2 * ahead + c), kv_send, kv_recv.at[ahead - 1],
            chip_device(rotated(chip, ahead), c, z),
        ).start()

    send_kv(1)

    weight[chip] = out_weight[...]

    def spread(u):
        block = weight.at[4 * y + u]
        for way, step in enumerate((1, 3)):
            remote(
                block, block, weight_send, plane_recv.at[way], device((y + step) % 4, x, c, z)
            ).start()

    for way, step in enumerate((1, 3)):
        block = weight.at[chip]
        remote(
            block, block, weight_send, line_recv.at[way], device(y, (x + step) % 4, c, z)
        ).start()
    spread(x)
    send_kv(2)

    def line_step():
        for way, step in enumerate((1, 3)):
            wait_bytes(weight.at[0], line_recv.at[way])
            came = (x - step + 4) % 4
            part = weight.at[4 * y + came, pl.ds(512 * way, 512)]
            remote(
                part, part, weight_send, line_fwd.at[way], device(y, (x + step) % 4, c, z)
            ).start()
            spread(came)

    def line_end():
        for way in (0, 1):
            wait_bytes(weight.at[0, pl.ds(0, 512)], line_fwd.at[way])
        spread((x + 2) % 4)

    def plane_step(way):
        step = (1, 3)[way]
        wait_bytes(weight.at[pl.ds(0, 4)], plane_recv.at[way])
        came = (y - step + 4) % 4
        part = weight.at[pl.ds(4 * came, 4), pl.ds(512 * way, 512)]
        remote(
            part, part, weight_send, plane_fwd.at[way], device((y + step) % 4, x, c, z)
        ).start()

    def plane_end():
        for way in (0, 1):
            wait_bytes(weight.at[pl.ds(0, 4), pl.ds(0, 512)], plane_fwd.at[way])

    def hand_over(slot, sem):
        remote(kv_slot(slot), kv_slot(slot), kv_send, kv_recv.at[sem], partner).start()

    pl.when(c == 0)(lambda: hand_over(4, 2))
    ends = []
    total_len = doc_lengths[0]
    for i in range(doc_lengths.shape[0]):
        if i:
            total_len = total_len + doc_lengths[i]
        ends.append(total_len)
    factor = HEAD_DIM ** (-0.5) * 1.4426950408889634

    def row_of(j):
        return (y + (0, 3, 1, 2)[j]) % 4

    def term(i, j):
        columns = [weight[4 * row_of(j) + u] for u in range(4)]
        return jnp.dot(
            att[i].reshape(256, 1024), jnp.concatenate(columns, axis=1),
            preferred_element_type=jnp.float32,
        )

    def put(i, j, value):
        at = (i * 4 + row_of(j)) * 2
        stage[pl.ds(at, 2)] = value.astype(jnp.bfloat16).reshape(2, 128, 512)
        return at

    up, down = (z + 1) % 4, (z + 3) % 4

    def deliver(i, j, value):
        at = put(i, j, value)
        for tc in (0, 1):
            remote(
                stage.at[at + tc], fin.at[((i - 1) * 2 + c) * 4 + row_of(j)], term_send, fin_recv,
                device(y, x, tc, (up, down)[i - 1]),
            ).start()

    def relay_out(j):
        at = put(0, j, term(0, j))
        remote(
            stage.at[pl.ds(at, 2)], relay.at[pl.ds(2 * row_of(j), 2)], term_send, relay_recv.at[j],
            device(y, x, c, (up, down)[j % 2]),
        ).start()

    def direct(i, j):
        deliver(i, j, term(i, j))

    def relayed(i, j):
        value = term(i, j)
        wait_bytes(relay.at[pl.ds(0, 2)], relay_recv.at[j])
        passed = relay[pl.ds(2 * row_of(j), 2)].reshape(256, 512)
        deliver(i, j, value + passed.astype(jnp.float32))

    def keep(j):
        at = put(3, j, term(3, j))
        spot = (4 + c) * 4 + row_of(j)
        fin[spot] = stage[at + c]
        remote(stage.at[at + 1 - c], fin.at[spot], term_send, fin_recv, partner).start()

    def after_far():
        wait_bytes(stage.at[pl.ds(0, 2)], att_recv.at[0])
        relay_out(0)
        plane_step(0)
        plane_step(1)
        relay_out(1)
        relay_out(2)

    def after_up():
        wait_bytes(stage.at[pl.ds(0, 2)], att_recv.at[1])
        relayed(1, 0)
        direct(1, 1)

    def after_down():
        wait_bytes(stage.at[pl.ds(0, 2)], att_recv.at[2])
        direct(2, 0)
        direct(2, 2)
        relayed(2, 1)
        relayed(1, 2)

    def after_own():
        wait_bytes(stage.at[pl.ds(0, 2)], att_recv.at[3])
        plane_end()
        relay_out(3)
        direct(1, 3)
        for j in range(4):
            keep(j)
        relayed(2, 3)

    def attend(slots, first, last):
        held = [kv_slot(slot) for slot in slots]
        starts = [(chip - 2) * 2 * SHARD + slot * SHARD for slot in slots]

        def block(i, carry):
            b = (z + jnp.where(i == 2, 3, jnp.where(i == 3, 0, 2 - i))) % 4
            pos = (chip * 2 + c) * SHARD + b * 128 + lax.broadcasted_iota(jnp.int32, (128, 1), 0)
            low = jnp.zeros((128, 1), jnp.int32)
            for end in ends:
                low = jnp.where(pos >= end, end, low)
            low = jnp.concatenate([low, low], axis=0)
            high = jnp.concatenate([pos, pos], axis=0)

            def heads(hp):
                n = i * 4 + hp
                lanes = hp * 256
                both = queries[pl.ds(pl.multiple_of(b * 128, 128), 128), pl.ds(lanes, 256)]
                q = jnp.concatenate([both[:, 0:128], both[:, 128:256]], axis=0)
                at = lax.broadcasted_iota(jnp.int32, (256, SHARD), 1)
                scores, top = [], None
                for ref, start in zip(held, starts):
                    part = lax.dot_general(
                        q, ref[:, 0:HEAD_DIM], (((1,), (1,)), ((), ())),
                        preferred_element_type=jnp.float32,
                    )
                    seen = at >= low - start
                    if first:
                        seen = seen & (at <= high - start)
                    part = jnp.where(seen, part, NEG_FILL)
                    peak = jnp.max(part, axis=1, keepdims=True)
                    top = peak if top is None else jnp.maximum(top, peak)
                    scores.append(part)
                if not first:
                    old = tops[n][:, 0:1]
                    top = jnp.maximum(top, old)
                    shrink = jnp.exp2((old - top) * factor)
                    total = totals[n][:, 0:1] * shrink
                    got = sums[n] * shrink
                for part, ref in zip(scores, held):
                    weights = jnp.exp2((part - top) * factor)
                    more = jnp.sum(weights, axis=1, keepdims=True)
                    value = jnp.dot(
                        weights.astype(jnp.bfloat16), ref[:, HEAD_DIM : 2 * HEAD_DIM],
                        preferred_element_type=jnp.float32,
                    )
                    if first:
                        total, got = more, value
                    else:
                        total, got = total + more, got + value
                if not last:
                    tops[n] = jnp.broadcast_to(top, (256, 128))
                    totals[n] = jnp.broadcast_to(total, (256, 128))
                    sums[n] = got
                else:
                    got = (got / total).astype(jnp.bfloat16)
                    att[i, c, :, pl.ds(lanes, 256)] = jnp.concatenate(
                        [got[0:128], got[128:256]], axis=1
                    )

            for hp in range(4):
                heads(hp)
                if last and hp == 1:
                    for k, then in enumerate((after_far, after_up, after_down)):
                        pl.when(i == k + 1)(then)
            if last:
                remote(att.at[i, c], att.at[i, c], att_send, att_recv.at[i], partner).start()
            return carry

        lax.fori_loop(0, 4, block, 0)

    attend([4 + c], True, False)
    line_step()
    wait_bytes(kv_slot(0), kv_recv.at[0])
    hand_over(2 + c, 3)
    wait_bytes(kv_slot(0), kv_recv.at[3])
    attend([2, 3], False, False)
    line_end()
    wait_bytes(kv_slot(0), kv_recv.at[1])
    pl.when(c == 1)(lambda: hand_over(1, 2))
    wait_bytes(kv_slot(0), kv_recv.at[2])
    attend([jnp.where(c == 0, 0, 4), 1], False, True)
    after_own()
    wait_bytes(fin.at[pl.ds(0, 20)], fin_recv)
    squares = jnp.zeros((128, HEAD_DIM), jnp.float32)
    for cs in (0, 1):
        for k in range(16):
            r, u = k // 4, k % 4
            lanes = slice((2 * k + cs) * 128, (2 * k + cs + 1) * 128)
            value = residual[:, lanes].astype(jnp.float32)
            for side in range(3):
                value = value + fin[
                    (side * 2 + cs) * 4 + r, :, u * 128 : (u + 1) * 128
                ].astype(jnp.float32)
            hidden[:, lanes] = value
            squares = squares + value * value
    variance = jnp.sum(squares, axis=1, keepdims=True) * (1.0 / D)
    shrink = lax.rsqrt(variance + 1e-06)
    for first in range(0, D, CHUNK):
        lanes = slice(first, first + CHUNK)
        normed[:, lanes] = (hidden[:, lanes] * shrink * gain[:, lanes]).astype(jnp.bfloat16)

    for _ in range(4):
        wait_bytes(kv_slot(0), kv_send)
    wait_bytes(weight.at[pl.ds(0, 15)], weight_send)
    wait_bytes(stage.at[pl.ds(0, 8)], att_send)
    wait_bytes(stage.at[pl.ds(0, 28)], term_send)


def front(queries, keys, values, doc_lengths, out_weight, residual, norm_gain):
    vmem = pl.BlockSpec(memory_space=pltpu.VMEM)
    dma = pltpu.SemaphoreType.DMA
    tokens = residual.shape[0]
    return pl.pallas_call(
        front_kernel,
        out_shape=(
            jax.ShapeDtypeStruct((tokens, D), jnp.bfloat16),
            jax.ShapeDtypeStruct((tokens, D), jnp.float32),
        ),
        in_specs=[pl.BlockSpec(memory_space=pltpu.SMEM)] + [vmem] * 6,
        out_specs=(vmem, vmem),
        scratch_shapes=[
            pltpu.VMEM((6 * SHARD, 2 * HEAD_DIM), jnp.bfloat16),
            pltpu.VMEM((16, 1024, HEAD_DIM), jnp.bfloat16),
            pltpu.VMEM((4, 2, 128, 1024), jnp.bfloat16),
            pltpu.VMEM((8, 128, 512), jnp.bfloat16),
            pltpu.VMEM((32, 128, 512), jnp.bfloat16),
            pltpu.VMEM((24, 128, 512), jnp.bfloat16),
            pltpu.VMEM((16, 256, 128), jnp.float32),
            pltpu.VMEM((16, 256, 128), jnp.float32),
            pltpu.VMEM((16, 256, 128), jnp.float32),
            dma, dma((4,)), dma((2,)), dma((2,)), dma((2,)), dma((2,)), dma,
            dma, dma((4,)), dma((4,)), dma, dma,
        ],
        compiler_params=pltpu.CompilerParams(
            has_side_effects=True, vmem_limit_bytes=60 * 1024 * 1024, collective_id=1
        ),
        cost_estimate=pl.CostEstimate(
            flops=10**10, bytes_accessed=10**7, transcendentals=10**7
        ),
    )(doc_lengths, queries, keys, values, out_weight, residual, norm_gain.reshape(1, D))


def body(
    queries, keys, values, doc_lengths, out_weight, residual, norm_gain, expert_ids,
    gate_values, w_gate, w_up, w_down,
):
    normed, hidden = front(queries, keys, values, doc_lengths, out_weight, residual, norm_gain)
    return routed_layer(normed, hidden, expert_ids, gate_values, w_gate, w_up, w_down)


def solution(mesh):
    in_specs = (
        P("seq", "exp"),
        P("seq", "exp"),
        P("seq", "exp"),
        P(),
        P("exp", "seq"),
        P(("seq", "exp"), None),
        P(),
        P(("seq", "exp"), None),
        P(("seq", "exp"), None),
        P(("seq", "exp"), None, None),
        P(("seq", "exp"), None, None),
        P(("seq", "exp"), None, None),
    )
    out_specs = P(("seq", "exp"), None)
    return jax.shard_map(body, mesh=mesh, in_specs=in_specs, out_specs=out_specs, check_vma=False)
```
